128 devices in a mesh: head: 8 (over z_hi, x), ctx: 16 (over z_lo, y, core).
Axes of the slice: x: 4, y: 4, z: 4 (z_hi: 2, z_lo: 2; z = z_hi * 2 + z_lo), core: 2. Of those that a mesh axis runs over, the one named last changes fastest.
Arguments:
- mla_queries: bfloat16 [128, 128, 576], P('head'), may hold values from -4 to 4
- latent_cache: bfloat16 [65536, 576], P('ctx'), may hold values from -4 to 4
- normalizers: float32 [128, 128], P('head'), may hold values from 9 to 15
- query_positions: int32 [128], replicated, may hold values from 0 to 131071, as said below
- key_positions: int32 [65536], P('ctx'), may hold values from 0 to 131071, as said below
- index_queries: bfloat16 [64, 128, 128], P('head'), may hold values from -24 to 24
- index_keys: bfloat16 [65536, 128], P(('ctx', 'head')), may hold values from -24 to 24
- index_weights: bfloat16 [64, 128], P('head'), may hold values from -16 to 16
Outputs:
- grad_queries: float32 [64, 128, 128], P('head')
- grad_weights: float32 [64, 128], P('head')
- grad_keys: float32 [65536, 128], P(('ctx', 'head'))
The draws below stay inside these ranges and needn't reach their ends.
Inputs may be any that keep to these rules, and one draw needn't show every extreme that they name: `query_positions`: every query position is one the keys' positions could reach. `key_positions`: key positions rise strictly along the keys.
All inputs are finite; a program needn't handle non-finite values.
Results may differ from the reference program's by a relative error of at most 0.00115.
The reference program's roundings to bfloat16 on the way (of `pre_grad`) count: a program that leaves them out, or rounds other values in their place, can miss the bound.
Values may be sent and summed in bfloat16 or wider, within the bound.
No kernel may reach another device: no remote copies, remote signals or barrier semaphores. Data moves between devices by JAX's collectives and lax.ppermute only.
A program may use at most 128 MiB of HBM per device.

```python
import math
import jax
import jax.numpy as jnp
from jax import lax

H = 128
D_LAT = 512
D_ROPE = 64
HI = 64
DI = 128
QUERIES = 128
KEYS = 65536


def indexer_parts(key):
    folded = jax.random.fold_in(key, 17)
    streams = jax.random.split(folded, 4)
    raw_keys = jax.random.normal(streams[0], (KEYS, DI), jnp.float32)
    queries = jax.random.normal(streams[1], (HI, QUERIES, DI), jnp.float32)
    weights = 3.0 * jax.random.normal(streams[2], (HI, QUERIES), jnp.float32)
    scales = jnp.exp(jax.random.uniform(streams[3], (KEYS, 1), jnp.float32, math.log(0.7), math.log(1.4)))
    index_rows = raw_keys * scales
    return (jnp.clip(index_rows, -24.0, 24.0), jnp.clip(queries, -24.0, 24.0), jnp.clip(weights, -16.0, 16.0))


def draw_index_keys(key, part):
    return indexer_parts(key)[0].astype(jnp.bfloat16)


def draw_index_queries(key, part):
    return indexer_parts(key)[1].astype(jnp.bfloat16)


def draw_index_weights(key, part):
    return indexer_parts(key)[2].astype(jnp.bfloat16)


def draw_query_positions(key, part):
    first_stream, second_stream = jax.random.split(jax.random.fold_in(key, 11))
    spread = jax.random.randint(first_stream, (QUERIES,), 0, 2 * KEYS)
    late = jax.random.randint(second_stream, (4,), KEYS, 2 * KEYS)
    spread = spread.at[QUERIES - 4:].set(late)
    spread = spread.at[0].set(0).at[QUERIES - 1].set(2 * KEYS - 1)
    return spread.astype(jnp.int32)


def draw_key_positions(key, part):
    extra = jax.random.randint(jax.random.fold_in(key, 13), (KEYS,), 0, 2)
    extra = extra.at[0].set(0).at[KEYS - 1].set(1)
    return (2 * jnp.arange(KEYS, dtype=jnp.int32) + extra).astype(jnp.int32)


def steps_of(own_key, dims, cuts, smallest, high):
    level, own = 1.0, jax.random.fold_in(own_key, 6)
    for dim, shards_of in cuts:
        draws = jnp.exp(jax.random.uniform(jax.random.fold_in(own, dim), (shards_of,), jnp.float32, smallest / len(cuts), high / len(cuts)))
        level = level * jnp.repeat(draws, dims[dim] // shards_of).reshape([-1 if axis == dim else 1 for axis in range(len(dims))])
    return level


def gaussian(rng, shape, width, bound, cuts=(), held_as=jnp.bfloat16):
    values = width * jax.random.normal(rng, shape, jnp.float32)
    if cuts:
        values = values * steps_of(rng, shape, cuts, -0.22, 0.18)
    return jnp.clip(values, -bound, bound).astype(held_as)


def setup_inputs(seed: int = 0) -> dict:
    key_list = jax.random.split(jax.random.key(seed), 9)
    mla_queries = gaussian(key_list[0], (H, QUERIES, D_LAT + D_ROPE), 1.0, 4.0, ((0, 8),))
    latent_cache = gaussian(key_list[1], (KEYS, D_LAT + D_ROPE), 1.0, 4.0, ((0, 16),))
    normalizers = jnp.clip(9.0 + 6.0 * jax.random.uniform(key_list[2], (H, QUERIES), jnp.float32) ** steps_of(key_list[2], (H, QUERIES), ((0, 8),), -0.2, 0.2), 9.0, 15.0)
    query_positions = draw_query_positions(jax.random.fold_in(key_list[8], 71), 0)
    key_positions = draw_key_positions(jax.random.fold_in(key_list[8], 71), 0)
    index_queries = draw_index_queries(jax.random.fold_in(key_list[8], 71), 0)
    index_keys = draw_index_keys(jax.random.fold_in(key_list[8], 71), 0)
    index_weights = draw_index_weights(jax.random.fold_in(key_list[8], 71), 0)
    return {"mla_queries": mla_queries, "latent_cache": latent_cache, "normalizers": normalizers, "query_positions": query_positions, "key_positions": key_positions, "index_queries": index_queries, "index_keys": index_keys, "index_weights": index_weights}


att_scale = 192.0 ** -0.5
loss_scale = 1024.0
masked_floor = -1.0e30


def reference(mla_queries, latent_cache, normalizers, query_positions, key_positions, index_queries, index_keys, index_weights):
    head_total = mla_queries.shape[0]
    query_count = mla_queries.shape[1]
    query_flat = mla_queries.reshape(head_total * query_count, mla_queries.shape[2])
    key_total = latent_cache.shape[0]
    block_rows = math.gcd(key_total, 1024)
    block_count = key_total // block_rows

    def probability_block(block_index):
        first_row = block_index * block_rows
        cache_rows = lax.dynamic_slice_in_dim(latent_cache, first_row, block_rows, 0)
        positions = lax.dynamic_slice_in_dim(key_positions, first_row, block_rows, 0)
        scores = jnp.dot(cache_rows, query_flat.T, preferred_element_type=jnp.float32)
        scores = scores.reshape(block_rows, head_total, query_count)
        weights = jnp.exp(scores * att_scale - normalizers[None])
        visible = positions[:, None] <= query_positions[None, :]
        return jnp.where(visible, jnp.sum(weights, axis=1), 0.0)

    block_ids = jnp.arange(block_count, dtype=jnp.int32)
    summed_probs = lax.map(probability_block, block_ids).reshape(key_total, query_count)

    index_heads = index_queries.shape[0]
    index_width = index_queries.shape[2]
    pair_flat = index_queries.reshape(index_heads * query_count, index_width)
    index_scale = (index_heads * index_width) ** -0.5
    weights_float = index_weights.astype(jnp.float32)

    def logit_block(block_index):
        first_row = block_index * block_rows
        key_rows = lax.dynamic_slice_in_dim(index_keys, first_row, block_rows, 0)
        relu_input = jnp.dot(key_rows, pair_flat.T, preferred_element_type=jnp.float32)
        relu_input = relu_input.reshape(block_rows, index_heads, query_count)
        return index_scale * jnp.sum(jnp.maximum(relu_input, 0.0) * weights_float[None], axis=1)

    logits = lax.map(logit_block, block_ids).reshape(key_total, query_count)
    visible_all = key_positions[:, None] <= query_positions[None, :]
    hidden_logits = jnp.where(visible_all, logits, masked_floor)
    row_max = jnp.max(hidden_logits, axis=0)
    exp_terms = jnp.where(visible_all, jnp.exp(hidden_logits - row_max[None]), 0.0)
    softmax_probs = exp_terms / jnp.sum(exp_terms, axis=0)[None]
    target = summed_probs / jnp.sum(summed_probs, axis=0)[None]
    logit_grad = loss_scale * jnp.where(visible_all, softmax_probs - target, 0.0)

    def gradient_block(carry, block_index):
        grad_query_sum, grad_weight_sum = carry
        first_row = block_index * block_rows
        key_rows = lax.dynamic_slice_in_dim(index_keys, first_row, block_rows, 0)
        grad_rows = lax.dynamic_slice_in_dim(logit_grad, first_row, block_rows, 0)
        relu_input = jnp.dot(key_rows, pair_flat.T, preferred_element_type=jnp.float32)
        relu_input = relu_input.reshape(block_rows, index_heads, query_count)
        gradient_gate = jnp.where(relu_input > 0.0, index_scale * weights_float[None], 0.0)
        pre_grad = (gradient_gate * grad_rows[:, None, :]).astype(jnp.bfloat16)
        pre_flat = pre_grad.reshape(block_rows, index_heads * query_count)
        query_term = jnp.dot(pre_flat.T, key_rows, preferred_element_type=jnp.float32)
        grad_query_sum = grad_query_sum + query_term.reshape(index_heads, query_count, index_width)
        grad_weight_sum = grad_weight_sum + jnp.sum(jnp.maximum(relu_input, 0.0) * grad_rows[:, None, :], axis=0)
        key_term = jnp.dot(pre_flat, pair_flat, preferred_element_type=jnp.float32)
        return (grad_query_sum, grad_weight_sum), key_term

    start_carry = (jnp.zeros((index_heads, query_count, index_width), jnp.float32), jnp.zeros((index_heads, query_count), jnp.float32))
    final_carry, key_blocks = lax.scan(gradient_block, start_carry, block_ids)
    grad_queries = final_carry[0]
    grad_weights = index_scale * final_carry[1]
    grad_keys = key_blocks.reshape(key_total, index_width)
    return (grad_queries, grad_weights, grad_keys)
```

```python
import functools
import math

import jax
import jax.numpy as jnp
from jax import lax
from jax.experimental import pallas as pl
from jax.experimental.pallas import tpu as pltpu
from jax.sharding import Mesh
from jax.sharding import PartitionSpec as P

att_scale = 192.0 ** (-0.5)
loss_scale = 1024.0
masked_floor = -1e30
log2e = math.log2(math.e)
chunks = 2

NT = (((1,), (1,)), ((), ()))
NN = (((1,), (0,)), ((), ()))
f32 = jnp.float32
bf16 = jnp.bfloat16


def dot(a, b, dims=NN):
    return lax.dot_general(a, b, dims, preferred_element_type=f32)


def visible_mask(kp_row, qp_row):
    n = kp_row.shape[1]
    q = qp_row.shape[1]
    kp = jnp.transpose(jnp.broadcast_to(kp_row, (q, n)))
    return kp <= jnp.broadcast_to(qp_row, (n, q))


def params(mb=40):
    return pltpu.CompilerParams(vmem_limit_bytes=mb * 1024 * 1024)


def probs_kernel(cache, q, nrm, kp, qp, out, tot):
    rows = cache.shape[0]
    heads, queries = nrm.shape
    x = cache[...]
    acc = jnp.zeros((rows, queries), f32)
    for pair in range(heads // 2):
        s = dot(x, q[pl.ds(pair * 2 * queries, 2 * queries), :], NT)
        for u in range(2):
            n = nrm[pl.ds(pair * 2 + u, 1), :] * log2e
            acc += jnp.exp2(s[:, u * queries : (u + 1) * queries] * (att_scale * log2e) - n)
    acc = jnp.where(visible_mask(kp[0], qp[...]), acc, 0.0)
    out[0] = acc

    @pl.when(pl.program_id(0) == 0)
    def _():
        tot[...] = jnp.zeros(tot.shape, f32)

    tot[...] += jnp.broadcast_to(jnp.sum(acc, axis=0, keepdims=True), tot.shape)


def probs_chunk(c, cache, q, nrm, kp, qp, parts):
    keys, width = cache.shape
    rows = keys // parts // chunks
    heads, queries = nrm.shape
    return pl.pallas_call(
        probs_kernel,
        grid=(parts,),
        in_specs=[
            pl.BlockSpec((rows, width), lambda d: (d * chunks + c, 0)),
            pl.BlockSpec(q.shape, lambda d: (0, 0)),
            pl.BlockSpec(nrm.shape, lambda d: (0, 0)),
            pl.BlockSpec((1, 1, rows), lambda d: (d * chunks + c, 0, 0)),
            pl.BlockSpec(qp.shape, lambda d: (0, 0)),
        ],
        out_specs=[
            pl.BlockSpec((1, rows, queries), lambda d: (d, 0, 0)),
            pl.BlockSpec((8, queries), lambda d: (0, 0)),
        ],
        out_shape=[
            jax.ShapeDtypeStruct((parts, rows, queries), f32),
            jax.ShapeDtypeStruct((8, queries), f32),
        ],
        compiler_params=params(),
        cost_estimate=pl.CostEstimate(
            flops=2 * parts * rows * q.shape[0] * width,
            bytes_accessed=parts * rows * width * 2 + q.size * 2,
            transcendentals=parts * rows * q.shape[0],
        ),
        name="probs",
    )(cache, q, nrm, kp.reshape(parts * chunks, 1, rows), qp)


def logits_kernel(scale, half_rows, keys, qa, qb, kp, qp, e_out, stats, acc):
    queries = qp.shape[1]
    step = pl.program_id(0)

    @pl.when(step == 0)
    def _():
        acc[...] = jnp.zeros(acc.shape, f32)

    k = keys[...]
    total = acc[...]
    for q in (qa, qb):
        for pair in range(half_rows // queries // 2):
            s = dot(k, q[0, pl.ds(pair * 2 * queries, 2 * queries), :], NT)
            w = q[0, pl.ds(half_rows, 16), :].astype(f32)
            for u in range(2):
                row = pair * 2 + u
                total += jnp.maximum(s[:, u * queries : (u + 1) * queries], 0.0) * w[row : row + 1]
    acc[...] = total

    @pl.when(step == pl.num_programs(0) - 1)
    def _():
        vis = visible_mask(kp[...], qp[...])
        hidden = jnp.where(vis, total * scale, masked_floor)
        m = jnp.max(hidden, axis=0, keepdims=True)
        e = jnp.where(vis, jnp.exp(hidden - m), 0.0)
        e_out[...] = e
        z = jnp.sum(e, axis=0, keepdims=True)
        rows = lax.broadcasted_iota(jnp.int32, stats.shape, 0)
        stats[...] = jnp.where(rows == 0, m, z)


def logits_call(keys, qa, qb, kp, qp, scale, half_rows):
    n, width = keys.shape
    parts, rows, _ = qa.shape
    queries = qp.shape[1]
    qspec = pl.BlockSpec((1, rows, width), lambda d: (d, 0, 0))
    full = lambda a: pl.BlockSpec(a.shape, lambda d: (0, 0))
    return pl.pallas_call(
        functools.partial(logits_kernel, scale, half_rows),
        grid=(parts,),
        in_specs=[full(keys), qspec, qspec, full(kp), full(qp)],
        out_specs=[
            pl.BlockSpec((n, queries), lambda d: (0, 0)),
            pl.BlockSpec((8, queries), lambda d: (0, 0)),
        ],
        out_shape=[
            jax.ShapeDtypeStruct((n, queries), f32),
            jax.ShapeDtypeStruct((8, queries), f32),
        ],
        scratch_shapes=[pltpu.VMEM((n, queries), f32)],
        compiler_params=params(),
        cost_estimate=pl.CostEstimate(
            flops=4 * 2 * n * parts * half_rows * width,
            bytes_accessed=parts * rows * width * 4,
            transcendentals=0,
        ),
        name="logits",
    )(keys, qa, qb, kp, qp)


def lg_kernel(*refs):
    recs = refs[:chunks]
    e, own, stats, kp, qp, lg = refs[chunks:]
    s = jnp.concatenate([jnp.sum(r[...], axis=0) for r in recs], axis=0)
    m_all, z_all, t_all = stats[:, 0, :], stats[:, 1, :], stats[:, 2, :]
    top = jnp.max(m_all, axis=0, keepdims=True)
    z = jnp.sum(z_all * jnp.exp(m_all - top), axis=0, keepdims=True)
    t = jnp.sum(t_all, axis=0, keepdims=True)
    p = e[...] * jnp.exp(own[0:1, :] - top) / z
    target = s / t
    lg[...] = loss_scale * jnp.where(visible_mask(kp[...], qp[...]), p - target, 0.0)


def lg_call(recs, e, own, stats, kp, qp):
    return pl.pallas_call(
        lg_kernel,
        out_shape=jax.ShapeDtypeStruct(e.shape, f32),
        compiler_params=params(),
        cost_estimate=pl.CostEstimate(
            flops=sum(r.size for r in recs), bytes_accessed=4 * sum(r.size for r in recs), transcendentals=0
        ),
        name="logit_grad",
    )(*recs, e, own, stats, kp, qp)


def grads_kernel(scale, half_rows, first, *refs):
    if first:
        keys, keys_t, lg_ref, q, out, gk = refs
    else:
        keys, keys_t, lg_ref, q, gk_in, out, gk = refs
    queries = lg_ref.shape[1]
    width = keys.shape[1]
    half = width // 2

    @pl.when(pl.program_id(0) == 0)
    def _():
        gk[...] = jnp.zeros(gk.shape, f32) if first else gk_in[...]

    k = keys[...]
    lg = lg_ref[...]
    w = q[0, pl.ds(half_rows, 16), :].astype(f32) * scale
    for pair in range(half_rows // queries // 2):
        qp = q[0, pl.ds(pair * 2 * queries, 2 * queries), :]
        s = dot(k, qp, NT)
        pres = []
        for u in range(2):
            row = pair * 2 + u
            su = s[:, u * queries : (u + 1) * queries]
            pres.append(jnp.where(su > 0.0, w[row : row + 1] * lg, 0.0).astype(bf16))
            gw = scale * jnp.sum(jnp.maximum(su, 0.0) * lg, axis=0, keepdims=True)
            for v in range(2):
                out[row * 2 + v, pl.ds(half, 8), :] = jnp.broadcast_to(gw, (8, queries))
        pre = jnp.concatenate(pres, axis=1)
        gk[...] += dot(pre, qp)
        gq = dot(keys_t[...], pre)
        for u in range(2):
            for v in range(2):
                out[(pair * 2 + u) * 2 + v, pl.ds(0, half), :] = gq[
                    v * half : (v + 1) * half, u * queries : (u + 1) * queries
                ]


def grads_call(keys, keys_t, lg, q, gk_in, scale, half_rows):
    n, width = keys.shape
    parts, rows, _ = q.shape
    queries = lg.shape[1]
    per = 2 * half_rows // queries
    full = lambda a: pl.BlockSpec(a.shape, lambda d: (0, 0))
    first = gk_in is None
    args = [keys, keys_t, lg, q] + ([] if first else [gk_in])
    specs = [full(keys), full(keys_t), full(lg), pl.BlockSpec((1, rows, width), lambda d: (d, 0, 0))]
    specs += [] if first else [full(gk_in)]
    return pl.pallas_call(
        functools.partial(grads_kernel, scale, half_rows, first),
        grid=(parts,),
        in_specs=specs,
        out_specs=[
            pl.BlockSpec((per, width // 2 + 8, queries), lambda d: (d, 0, 0)),
            pl.BlockSpec((n, width), lambda d: (0, 0)),
        ],
        out_shape=[
            jax.ShapeDtypeStruct((parts * per, width // 2 + 8, queries), f32),
            jax.ShapeDtypeStruct((n, width), f32),
        ],
        compiler_params=params(),
        cost_estimate=pl.CostEstimate(
            flops=3 * 2 * n * parts * half_rows * width,
            bytes_accessed=parts * rows * width * 6,
            transcendentals=0,
        ),
        name="grads",
    )(*args)


def sum_kernel(rec, out):
    total = jnp.sum(rec[...], axis=0)
    for i in range(out.shape[0]):
        out[i] = total


def sum_call(rec, copies):
    return pl.pallas_call(
        sum_kernel,
        out_shape=jax.ShapeDtypeStruct((copies,) + rec.shape[1:], f32),
        compiler_params=params(),
        name="sum_parts",
    )(rec)


def place_kernel(rec, gq, gw):
    heads, _, width = gq.shape
    half = width // 2
    for j in range(heads):
        core, jj = j // (heads // 2), j % (heads // 2)
        lo, hi = (jj * 2) * 2 + core, (jj * 2 + 1) * 2 + core
        both = jnp.concatenate([rec[lo, pl.ds(0, half), :], rec[hi, pl.ds(0, half), :]], axis=0)
        gq[j] = jnp.transpose(both)
        gw[pl.ds(j, 1), :] = rec[lo, pl.ds(half, 1), :]


def place_call(rec, heads, width):
    queries = rec.shape[2]
    return pl.pallas_call(
        place_kernel,
        out_shape=[
            jax.ShapeDtypeStruct((heads, queries, width), f32),
            jax.ShapeDtypeStruct((heads, queries), f32),
        ],
        compiler_params=params(),
        name="place",
    )(rec)


def spread(x, axes, count):
    return lax.all_to_all(jnp.broadcast_to(x[None], (count,) + x.shape), axes, 0, 0, tiled=True)


def per_device(
    mla_queries,
    latent_cache,
    normalizers,
    query_positions,
    key_positions,
    index_queries,
    index_keys,
    index_weights,
):
    head_count, query_count, _ = mla_queries.shape
    query_flat = mla_queries.reshape(head_count * query_count, mla_queries.shape[2])
    sub_keys, index_width = index_keys.shape
    parts = lax.axis_size("head")
    zy = lax.axis_size("zy")
    local_heads = index_queries.shape[0]
    half_heads = local_heads // 2
    half_rows = half_heads * query_count
    index_scale = (local_heads * parts * index_width) ** (-0.5)
    core = lax.axis_index("core")
    swap = [(0, 1), (1, 0)]
    qp = query_positions.reshape(1, query_count)

    own_q = lax.dynamic_slice_in_dim(index_queries, core * half_heads, half_heads, 0)
    own_w = lax.dynamic_slice_in_dim(index_weights, core * half_heads, half_heads, 0)
    own = jnp.concatenate(
        [
            own_q.reshape(half_rows, index_width),
            jnp.pad(own_w, ((0, 16 - half_heads), (0, 0))),
        ],
        axis=0,
    )
    q_mine = spread(own, "head", parts)
    q_other = lax.ppermute(q_mine, "core", swap)

    pieces = [
        probs_chunk(c, latent_cache, query_flat, normalizers, key_positions, qp, parts) for c in range(chunks)
    ]
    recs = [lax.all_to_all(s, "head", 0, 0, tiled=True) for s, _ in pieces]

    offset = lax.axis_index("head") * sub_keys
    own_kp = lax.dynamic_slice_in_dim(key_positions, offset, sub_keys, 0).reshape(1, sub_keys)
    e, local = logits_call(index_keys, q_mine, q_other, own_kp, qp, index_scale, half_rows)
    target_total = sum(t for _, t in pieces)[0:1]
    stats = jnp.concatenate([local[0:2], target_total, target_total], axis=0)
    all_stats = spread(stats, ("head", "zy", "core"), parts * zy * 2)
    lg = lg_call(recs, e, local, all_stats, own_kp, qp)

    keys_t = index_keys.T
    out_other, gk = grads_call(index_keys, keys_t, lg, q_other, None, index_scale, half_rows)
    got = lax.ppermute(out_other, "core", swap)
    out_mine, gk = grads_call(index_keys, keys_t, lg, q_mine, gk, index_scale, half_rows)
    block = lax.all_to_all(out_mine + got, ("head", "zy"), 0, 0, tiled=True)
    summed = sum_call(block, zy * 2)
    final = lax.all_to_all(summed, ("zy", "core"), 0, 0, tiled=True)
    gq, gw = place_call(final, local_heads, index_width)
    return gq, gw, gk


def solution(mesh):
    heads = mesh.shape["head"]
    ctx = mesh.shape["ctx"]
    fine = Mesh(mesh.devices.reshape(heads, ctx // 2, 2), ("head", "zy", "core"))
    split = ("zy", "core")
    placed = (
        P("head", None, None),
        P(split, None),
        P("head", None),
        P(),
        P(split),
        P("head", None, None),
        P(split + ("head",), None),
        P("head", None),
    )
    return jax.shard_map(
        per_device,
        mesh=fine,
        in_specs=placed,
        out_specs=(P("head", None, None), P("head", None), P(split + ("head",), None)),
        check_vma=False,
    )
```

```python
import functools
import math

import jax
import jax.numpy as jnp
from jax import lax
from jax.experimental import pallas as pl
from jax.experimental.pallas import tpu as pltpu
from jax.sharding import Mesh
from jax.sharding import PartitionSpec as P

att_scale = 192.0 ** (-0.5)
loss_scale = 1024.0
masked_floor = -1e30
log2e = math.log2(math.e)

NT = (((1,), (1,)), ((), ()))
NN = (((1,), (0,)), ((), ()))
f32 = jnp.float32
bf16 = jnp.bfloat16


def dot(a, b, dims=NN):
    return lax.dot_general(a, b, dims, preferred_element_type=f32)


def visible_mask(kp_row, qp_row):
    n = kp_row.shape[1]
    q = qp_row.shape[1]
    kp = jnp.transpose(jnp.broadcast_to(kp_row, (q, n)))
    return kp <= jnp.broadcast_to(qp_row, (n, q))


def params(mb=40):
    return pltpu.CompilerParams(vmem_limit_bytes=mb * 1024 * 1024)


def exponent(top):
    return jnp.clip(jnp.ceil(jnp.log2(jnp.maximum(top, 1e-37))), -122.0, 128.0)


def shrink(x, e):
    r = jnp.exp2(e * -0.5)
    return (x * r) * r


def grow(x, e):
    r = jnp.exp2(e * 0.5)
    return (x * r) * r


def to_code(x):
    return jnp.clip(jnp.floor(x + 0.5), -32768.0, 32767.0).astype(jnp.int32).astype(jnp.int16)


def from_code(c):
    return c.astype(jnp.int32).astype(f32)


def root_code(x, e):
    return to_code(jnp.sqrt(jnp.sqrt(shrink(x, e))) * 65535.0 - 32768.0)


def root_decode(c, e):
    r = (from_code(c) + 32768.0) * (1.0 / 65535.0) * jnp.exp2(e * 0.25)
    r = r * r
    return r * r


def probs_kernel(cache, q, nrm, kp, qp, out, tot, qt, nb):
    keys = cache.shape[1]
    heads, queries = nrm.shape

    @pl.when(pl.program_id(0) == 0)
    def _():
        tot[...] = jnp.zeros(tot.shape, f32)
        for h in range(heads):
            qt[pl.ds(h * queries, queries), :] = jnp.transpose(q[h])
            nb[h] = jnp.transpose(jnp.broadcast_to(nrm[pl.ds(h, 1), :] * log2e, (queries, queries)))

    x = cache[...]
    acc = [jnp.zeros((queries, queries), f32) for _ in range(keys // queries)]
    for pair in range(heads // 2):
        s = dot(qt[pl.ds(pair * 2 * queries, 2 * queries), :], x)
        for u in range(2):
            n = nb[pair * 2 + u]
            for i in range(len(acc)):
                block = s[u * queries : (u + 1) * queries, i * queries : (i + 1) * queries]
                acc[i] += jnp.exp2(block * (att_scale * log2e) - n)
    summed = jnp.concatenate([jnp.transpose(a) for a in acc], axis=0)
    summed = jnp.where(visible_mask(kp[0], qp[...]), summed, 0.0)
    e = exponent(jnp.max(summed, axis=0, keepdims=True))
    out[0, pl.ds(0, keys), :] = root_code(summed, e)
    out[0, pl.ds(keys, 16), :] = to_code(jnp.broadcast_to(e, (16, queries)))
    tot[...] += jnp.broadcast_to(jnp.sum(summed, axis=0, keepdims=True), tot.shape)


def probs_call(cache_t, q_t, nrm, kp, qp, parts):
    width, keys = cache_t.shape
    rows = keys // parts
    heads, queries = nrm.shape
    return pl.pallas_call(
        probs_kernel,
        grid=(parts,),
        in_specs=[
            pl.BlockSpec((width, rows), lambda d: (0, d)),
            pl.BlockSpec(q_t.shape, lambda d: (0, 0, 0)),
            pl.BlockSpec(nrm.shape, lambda d: (0, 0)),
            pl.BlockSpec((1, 1, rows), lambda d: (d, 0, 0)),
            pl.BlockSpec(qp.shape, lambda d: (0, 0)),
        ],
        out_specs=[
            pl.BlockSpec((1, rows + 16, queries), lambda d: (d, 0, 0)),
            pl.BlockSpec((8, queries), lambda d: (0, 0)),
        ],
        out_shape=[
            jax.ShapeDtypeStruct((parts, rows + 16, queries), jnp.int16),
            jax.ShapeDtypeStruct((8, queries), f32),
        ],
        scratch_shapes=[
            pltpu.VMEM((heads * queries, width), bf16),
            pltpu.VMEM((heads, queries, queries), f32),
        ],
        compiler_params=params(56),
        cost_estimate=pl.CostEstimate(
            flops=2 * keys * q_t.size,
            bytes_accessed=cache_t.size * 2 + q_t.size * 2,
            transcendentals=keys * heads * queries,
        ),
        name="probs",
    )(cache_t, q_t, nrm, kp.reshape(parts, 1, rows), qp)


def logits_kernel(scale, half_rows, keys, qa, qb, kp, qp, e_out, stats, acc):
    queries = qp.shape[1]
    step = pl.program_id(0)

    @pl.when(step == 0)
    def _():
        acc[...] = jnp.zeros(acc.shape, f32)

    k = keys[...]
    total = acc[...]
    for q in (qa, qb):
        for pair in range(half_rows // queries // 2):
            s = dot(k, q[0, pl.ds(pair * 2 * queries, 2 * queries), :], NT)
            w = q[0, pl.ds(half_rows, 16), :].astype(f32)
            for u in range(2):
                row = pair * 2 + u
                total += jnp.maximum(s[:, u * queries : (u + 1) * queries], 0.0) * w[row : row + 1]
    acc[...] = total

    @pl.when(step == pl.num_programs(0) - 1)
    def _():
        vis = visible_mask(kp[...], qp[...])
        hidden = jnp.where(vis, total * scale, masked_floor)
        m = jnp.max(hidden, axis=0, keepdims=True)
        e = jnp.where(vis, jnp.exp(hidden - m), 0.0)
        e_out[...] = e
        z = jnp.sum(e, axis=0, keepdims=True)
        rows = lax.broadcasted_iota(jnp.int32, stats.shape, 0)
        stats[...] = jnp.where(rows == 0, m, z)


def logits_call(keys, qa, qb, kp, qp, scale, half_rows):
    n, width = keys.shape
    parts, rows, _ = qa.shape
    queries = qp.shape[1]
    qspec = pl.BlockSpec((1, rows, width), lambda d: (d, 0, 0))
    full = lambda a: pl.BlockSpec(a.shape, lambda d: (0, 0))
    return pl.pallas_call(
        functools.partial(logits_kernel, scale, half_rows),
        grid=(parts,),
        in_specs=[full(keys), qspec, qspec, full(kp), full(qp)],
        out_specs=[
            pl.BlockSpec((n, queries), lambda d: (0, 0)),
            pl.BlockSpec((8, queries), lambda d: (0, 0)),
        ],
        out_shape=[
            jax.ShapeDtypeStruct((n, queries), f32),
            jax.ShapeDtypeStruct((8, queries), f32),
        ],
        scratch_shapes=[pltpu.VMEM((n, queries), f32)],
        compiler_params=params(),
        cost_estimate=pl.CostEstimate(
            flops=4 * 2 * n * parts * half_rows * width,
            bytes_accessed=parts * rows * width * 4,
            transcendentals=0,
        ),
        name="logits",
    )(keys, qa, qb, kp, qp)


def lg_kernel(rec, e, own, stats, kp, qp, lg):
    n = e.shape[0]
    s = jnp.zeros(e.shape, f32)
    for i in range(rec.shape[0]):
        ex = from_code(rec[i, pl.ds(n, 16), :])[0:1]
        s += root_decode(rec[i, pl.ds(0, n), :], ex)
    m_all, z_all, t_all = stats[:, 0, :], stats[:, 1, :], stats[:, 2, :]
    top = jnp.max(m_all, axis=0, keepdims=True)
    z = jnp.sum(z_all * jnp.exp(m_all - top), axis=0, keepdims=True)
    t = jnp.sum(t_all, axis=0, keepdims=True)
    p = e[...] * jnp.exp(own[0:1, :] - top) / z
    target = s / t
    lg[...] = loss_scale * jnp.where(visible_mask(kp[...], qp[...]), p - target, 0.0)


def lg_call(rec, e, own, stats, kp, qp):
    return pl.pallas_call(
        lg_kernel,
        out_shape=jax.ShapeDtypeStruct(e.shape, f32),
        compiler_params=params(),
        cost_estimate=pl.CostEstimate(flops=8 * rec.size, bytes_accessed=2 * rec.size, transcendentals=0),
        name="logit_grad",
    )(rec, e, own, stats, kp, qp)


def grads_kernel(scale, half_rows, first, *refs):
    if first:
        keys, keys_t, lg_ref, q, out, gk = refs
    else:
        keys, keys_t, lg_ref, q, gk_in, out, gk = refs
    queries = lg_ref.shape[1]
    width = keys.shape[1]
    half = width // 2

    @pl.when(pl.program_id(0) == 0)
    def _():
        gk[...] = jnp.zeros(gk.shape, f32) if first else gk_in[...]

    k = keys[...]
    lg = lg_ref[...]
    w = q[0, pl.ds(half_rows, 16), :].astype(f32) * scale
    for pair in range(half_rows // queries // 2):
        qp = q[0, pl.ds(pair * 2 * queries, 2 * queries), :]
        s = dot(k, qp, NT)
        pres = []
        for u in range(2):
            row = pair * 2 + u
            su = s[:, u * queries : (u + 1) * queries]
            pres.append(jnp.where(su > 0.0, w[row : row + 1] * lg, 0.0).astype(bf16))
            gw = scale * jnp.sum(jnp.maximum(su, 0.0) * lg, axis=0, keepdims=True)
            for v in range(2):
                out[row * 2 + v, pl.ds(half, 8), :] = jnp.broadcast_to(gw, (8, queries))
        pre = jnp.concatenate(pres, axis=1)
        gk[...] += dot(pre, qp)
        gq = dot(keys_t[...], pre)
        for u in range(2):
            for v in range(2):
                out[(pair * 2 + u) * 2 + v, pl.ds(0, half), :] = gq[
                    v * half : (v + 1) * half, u * queries : (u + 1) * queries
                ]


def grads_call(keys, keys_t, lg, q, gk_in, scale, half_rows):
    n, width = keys.shape
    parts, rows, _ = q.shape
    queries = lg.shape[1]
    per = 2 * half_rows // queries
    full = lambda a: pl.BlockSpec(a.shape, lambda d: (0, 0))
    first = gk_in is None
    args = [keys, keys_t, lg, q] + ([] if first else [gk_in])
    specs = [full(keys), full(keys_t), full(lg), pl.BlockSpec((1, rows, width), lambda d: (d, 0, 0))]
    specs += [] if first else [full(gk_in)]
    return pl.pallas_call(
        functools.partial(grads_kernel, scale, half_rows, first),
        grid=(parts,),
        in_specs=specs,
        out_specs=[
            pl.BlockSpec((per, width // 2 + 8, queries), lambda d: (d, 0, 0)),
            pl.BlockSpec((n, width), lambda d: (0, 0)),
        ],
        out_shape=[
            jax.ShapeDtypeStruct((parts * per, width // 2 + 8, queries), f32),
            jax.ShapeDtypeStruct((n, width), f32),
        ],
        compiler_params=params(),
        cost_estimate=pl.CostEstimate(
            flops=3 * 2 * n * parts * half_rows * width,
            bytes_accessed=parts * rows * width * 6,
            transcendentals=0,
        ),
        name="grads",
    )(*args)


def code_kernel(a, b, out):
    x = a[...] + b[...]
    half = x.shape[1] - 8
    queries = x.shape[2]
    for i in range(x.shape[0]):
        g = x[i, 0:half]
        e = exponent(jnp.max(jnp.abs(g), axis=0, keepdims=True))
        out[i, pl.ds(0, half), :] = to_code(shrink(g, e) * 32767.0)
        w = x[i, half : half + 8]
        ew = exponent(jnp.abs(w))
        fine = shrink(w, ew) * 32767.0
        hi = jnp.floor(fine + 0.5)
        lo = (fine - hi) * 65534.0
        e16 = jnp.broadcast_to(e, (16, queries))
        spare = jnp.concatenate([ew, ew], axis=0)
        row = lax.broadcasted_iota(jnp.int32, (16, queries), 0)
        spare = jnp.where(row == 0, e16, spare)
        spare = jnp.where(row == 2, jnp.concatenate([hi, hi], axis=0), spare)
        spare = jnp.where(row == 3, jnp.concatenate([lo, lo], axis=0), spare)
        out[i, pl.ds(half, 16), :] = to_code(spare)


def code_call(a, b, parts):
    n, rows, queries = a.shape
    per = n // parts
    spec = pl.BlockSpec((per, rows, queries), lambda d: (d, 0, 0))
    return pl.pallas_call(
        code_kernel,
        grid=(parts,),
        in_specs=[spec, spec],
        out_specs=pl.BlockSpec((per, rows + 8, queries), lambda d: (d, 0, 0)),
        out_shape=jax.ShapeDtypeStruct((n, rows + 8, queries), jnp.int16),
        compiler_params=params(),
        name="code_parts",
    )(a, b)


def sum_kernel(rec, out):
    half = rec.shape[1] - 16
    queries = rec.shape[2]
    g = jnp.zeros((half, queries), f32)
    w = jnp.zeros((1, queries), f32)
    for i in range(rec.shape[0]):
        spare = from_code(rec[i, pl.ds(half, 16), :])
        g += grow(from_code(rec[i, pl.ds(0, half), :]) * (1.0 / 32767.0), spare[0:1])
        w += grow((spare[2:3] + spare[3:4] * (1.0 / 65534.0)) * (1.0 / 32767.0), spare[1:2])
    for i in range(out.shape[0]):
        out[i, pl.ds(0, half), :] = g
        out[i, pl.ds(half, 8), :] = jnp.broadcast_to(w, (8, queries))


def sum_call(rec, copies):
    n, rows, queries = rec.shape
    return pl.pallas_call(
        sum_kernel,
        out_shape=jax.ShapeDtypeStruct((copies, rows - 8, queries), f32),
        compiler_params=params(),
        name="sum_parts",
    )(rec)


def place_kernel(rec, gq, gw):
    heads, _, width = gq.shape
    half = width // 2
    for j in range(heads):
        core, jj = j // (heads // 2), j % (heads // 2)
        lo, hi = (jj * 2) * 2 + core, (jj * 2 + 1) * 2 + core
        both = jnp.concatenate([rec[lo, pl.ds(0, half), :], rec[hi, pl.ds(0, half), :]], axis=0)
        gq[j] = jnp.transpose(both)
        gw[pl.ds(j, 1), :] = rec[lo, pl.ds(half, 1), :]


def place_call(rec, heads, width):
    queries = rec.shape[2]
    return pl.pallas_call(
        place_kernel,
        out_shape=[
            jax.ShapeDtypeStruct((heads, queries, width), f32),
            jax.ShapeDtypeStruct((heads, queries), f32),
        ],
        compiler_params=params(),
        name="place",
    )(rec)


def spread(x, axes, count):
    return lax.all_to_all(jnp.broadcast_to(x[None], (count,) + x.shape), axes, 0, 0, tiled=True)


def per_device(
    mla_queries,
    latent_cache,
    normalizers,
    query_positions,
    key_positions,
    index_queries,
    index_keys,
    index_weights,
):
    query_count = mla_queries.shape[1]
    sub_keys, index_width = index_keys.shape
    parts = lax.axis_size("head")
    zy = lax.axis_size("zy")
    local_heads = index_queries.shape[0]
    half_heads = local_heads // 2
    half_rows = half_heads * query_count
    index_scale = (local_heads * parts * index_width) ** (-0.5)
    core = lax.axis_index("core")
    swap = [(0, 1), (1, 0)]
    qp = query_positions.reshape(1, query_count)

    own_q = lax.dynamic_slice_in_dim(index_queries, core * half_heads, half_heads, 0)
    own_w = lax.dynamic_slice_in_dim(index_weights, core * half_heads, half_heads, 0)
    own = jnp.concatenate(
        [
            own_q.reshape(half_rows, index_width),
            jnp.pad(own_w, ((0, 16 - half_heads), (0, 0))),
        ],
        axis=0,
    )
    q_mine = spread(own, "head", parts)
    coded, totals = probs_call(
        latent_cache.T, mla_queries.transpose(0, 2, 1), normalizers, key_positions, qp, parts
    )
    q_mine, coded = lax.optimization_barrier((q_mine, coded))
    q_other = lax.ppermute(q_mine, "core", swap)
    rec = lax.all_to_all(coded, "head", 0, 0, tiled=True)

    offset = lax.axis_index("head") * sub_keys
    own_kp = lax.dynamic_slice_in_dim(key_positions, offset, sub_keys, 0).reshape(1, sub_keys)
    e, local = logits_call(index_keys, q_mine, q_other, own_kp, qp, index_scale, half_rows)
    stats = jnp.concatenate([local[0:2], totals[0:2]], axis=0)
    all_stats = spread(stats, ("head", "zy", "core"), parts * zy * 2)
    lg = lg_call(rec, e, local, all_stats, own_kp, qp)

    keys_t = index_keys.T
    out_other, gk = grads_call(index_keys, keys_t, lg, q_other, None, index_scale, half_rows)
    got = lax.ppermute(out_other, "core", swap)
    out_mine, gk = grads_call(index_keys, keys_t, lg, q_mine, gk, index_scale, half_rows)
    block = lax.all_to_all(code_call(out_mine, got, parts), ("head", "zy"), 0, 0, tiled=True)
    summed = sum_call(block, zy * 2)
    final = lax.all_to_all(summed, ("zy", "core"), 0, 0, tiled=True)
    gq, gw = place_call(final, local_heads, index_width)
    return gq, gw, gk


def solution(mesh):
    heads = mesh.shape["head"]
    ctx = mesh.shape["ctx"]
    fine = Mesh(mesh.devices.reshape(heads, ctx // 2, 2), ("head", "zy", "core"))
    split = ("zy", "core")
    placed = (
        P("head", None, None),
        P(split, None),
        P("head", None),
        P(),
        P(split),
        P("head", None, None),
        P(split + ("head",), None),
        P("head", None),
    )
    return jax.shard_map(
        per_device,
        mesh=fine,
        in_specs=placed,
        out_specs=(P("head", None, None), P("head", None), P(split + ("head",), None)),
        check_vma=False,
    )
```

```python
import functools
import math

import jax
import jax.numpy as jnp
from jax import lax
from jax.experimental import pallas as pl
from jax.experimental.pallas import tpu as pltpu
from jax.sharding import Mesh
from jax.sharding import PartitionSpec as P

att_scale = 192.0 ** (-0.5)
loss_scale = 1024.0
masked_floor = -1e30
log2e = math.log2(math.e)

NT = (((1,), (1,)), ((), ()))
NN = (((1,), (0,)), ((), ()))
f32 = jnp.float32
bf16 = jnp.bfloat16


def dot(a, b, dims=NN):
    return lax.dot_general(a, b, dims, preferred_element_type=f32)


def visible_mask(kp_row, qp_row):
    n = kp_row.shape[1]
    q = qp_row.shape[1]
    kp = jnp.transpose(jnp.broadcast_to(kp_row, (q, n)))
    return kp <= jnp.broadcast_to(qp_row, (n, q))


def params(mb=40):
    return pltpu.CompilerParams(vmem_limit_bytes=mb * 1024 * 1024)


def exponent(top):
    return jnp.clip(jnp.ceil(jnp.log2(jnp.maximum(top, 1e-37))), -122.0, 128.0)


def shrink(x, e):
    r = jnp.exp2(e * -0.5)
    return (x * r) * r


def grow(x, e):
    r = jnp.exp2(e * 0.5)
    return (x * r) * r


def to_code(x):
    return jnp.clip(jnp.floor(x + 0.5), -32768.0, 32767.0).astype(jnp.int32).astype(jnp.int16)


def from_code(c):
    return c.astype(jnp.int32).astype(f32)


def root_code(x, e):
    return to_code(jnp.sqrt(jnp.sqrt(shrink(x, e))) * 65535.0 - 32768.0)


def root_decode(c, e):
    r = (from_code(c) + 32768.0) * (1.0 / 65535.0) * jnp.exp2(e * 0.25)
    r = r * r
    return r * r


def probs_kernel(first, *refs):
    if first:
        cache, q, nrm, kp, qp, out, tot = refs
    else:
        cache, q, nrm, kp, qp, _, out, tot = refs
    keys = cache.shape[1]
    heads, queries = nrm.shape

    @pl.when(pl.program_id(0) == 0)
    def _():
        tot[...] = jnp.zeros(tot.shape, f32)

    rows = keys // 2
    sums = []
    xt = jnp.transpose(cache[...])
    for block in range(2):
        x = xt[block * rows : (block + 1) * rows]
        acc = jnp.zeros((rows, queries), f32)
        for pair in range(heads // 2):
            s = dot(x, jnp.concatenate([q[pair * 2], q[pair * 2 + 1]], axis=1))
            for u in range(2):
                n = nrm[pl.ds(pair * 2 + u, 1), :] * log2e
                acc += jnp.exp2(s[:, u * queries : (u + 1) * queries] * (att_scale * log2e) - n)
        sums.append(acc)
    summed = jnp.concatenate(sums, axis=0)
    summed = jnp.where(visible_mask(kp[0], qp[...]), summed, 0.0)
    e = exponent(jnp.max(summed, axis=0, keepdims=True))
    out[0, pl.ds(0, keys), :] = root_code(summed, e)
    out[0, pl.ds(keys, 16), :] = to_code(jnp.broadcast_to(e, (16, queries)))
    tot[...] += jnp.broadcast_to(jnp.sum(summed, axis=0, keepdims=True), tot.shape)


def probs_call(cache_t, q_t, nrm, kp, qp, parts, start, count, before):
    width, keys = cache_t.shape
    rows = keys // parts
    heads, queries = nrm.shape
    first = before is None
    args = [cache_t, q_t, nrm, kp.reshape(parts, 1, rows), qp] + ([] if first else [before])
    specs = [
        pl.BlockSpec((width, rows), lambda d: (0, d + start)),
        pl.BlockSpec(q_t.shape, lambda d: (0, 0, 0)),
        pl.BlockSpec(nrm.shape, lambda d: (0, 0)),
        pl.BlockSpec((1, 1, rows), lambda d: (d + start, 0, 0)),
        pl.BlockSpec(qp.shape, lambda d: (0, 0)),
    ] + ([] if first else [pl.BlockSpec(memory_space=pl.ANY)])
    return pl.pallas_call(
        functools.partial(probs_kernel, first),
        grid=(count,),
        in_specs=specs,
        out_specs=[
            pl.BlockSpec((1, rows + 16, queries), lambda d: (d + start, 0, 0)),
            pl.BlockSpec((8, queries), lambda d: (0, 0)),
        ],
        out_shape=[
            jax.ShapeDtypeStruct((parts, rows + 16, queries), jnp.int16),
            jax.ShapeDtypeStruct((8, queries), f32),
        ],
        input_output_aliases={} if first else {5: 0},
        compiler_params=params(56),
        cost_estimate=pl.CostEstimate(
            flops=2 * rows * count * q_t.size,
            bytes_accessed=cache_t.size * 2 * count // parts + q_t.size * 2,
            transcendentals=rows * count * heads * queries,
        ),
        name="probs",
    )(*args)


def logits_kernel(scale, half_rows, first, *refs):
    if first:
        keys, q, acc = refs
    else:
        keys, q, before, kp, qp, e_out, stats, acc = refs
    queries = acc.shape[1]
    step = pl.program_id(0)

    @pl.when(step == 0)
    def _():
        acc[...] = jnp.zeros(acc.shape, f32) if first else before[...]

    k = keys[...]
    total = acc[...]
    w = q[0, pl.ds(half_rows, 16), :].astype(f32)
    for pair in range(half_rows // queries // 2):
        s = dot(k, q[0, pl.ds(pair * 2 * queries, 2 * queries), :], NT)
        for u in range(2):
            row = pair * 2 + u
            total += jnp.maximum(s[:, u * queries : (u + 1) * queries], 0.0) * w[row : row + 1]
    acc[...] = total
    if first:
        return

    @pl.when(step == pl.num_programs(0) - 1)
    def _():
        vis = visible_mask(kp[...], qp[...])
        hidden = jnp.where(vis, acc[...] * scale, masked_floor)
        m = jnp.max(hidden, axis=0, keepdims=True)
        e = jnp.where(vis, jnp.exp(hidden - m), 0.0)
        e_out[...] = e
        z = jnp.sum(e, axis=0, keepdims=True)
        rows = lax.broadcasted_iota(jnp.int32, stats.shape, 0)
        stats[...] = jnp.where(rows == 0, m, z)


def logits_call(keys, q, before, kp, qp, scale, half_rows):
    n, width = keys.shape
    parts, rows, _ = q.shape
    queries = qp.shape[1]
    full = lambda a: pl.BlockSpec(a.shape, lambda d: (0, 0))
    first = before is None
    whole = pl.BlockSpec((n, queries), lambda d: (0, 0))
    args = [keys, q] + ([] if first else [before, kp, qp])
    specs = [full(keys), pl.BlockSpec((1, rows, width), lambda d: (d, 0, 0))]
    specs += [] if first else [full(before), full(kp), full(qp)]
    table = jax.ShapeDtypeStruct((n, queries), f32)
    return pl.pallas_call(
        functools.partial(logits_kernel, scale, half_rows, first),
        grid=(parts,),
        in_specs=specs,
        out_specs=whole if first else [whole, pl.BlockSpec((8, queries), lambda d: (0, 0))],
        out_shape=table if first else [table, jax.ShapeDtypeStruct((8, queries), f32)],
        scratch_shapes=[] if first else [pltpu.VMEM((n, queries), f32)],
        compiler_params=params(),
        cost_estimate=pl.CostEstimate(
            flops=2 * 2 * n * parts * half_rows * width,
            bytes_accessed=parts * rows * width * 2,
            transcendentals=0,
        ),
        name="logits",
    )(*args)


def lg_kernel(rec, e, own, stats, kp, qp, lg):
    n = e.shape[0]
    s = jnp.zeros(e.shape, f32)
    for i in range(rec.shape[0]):
        ex = from_code(rec[i, pl.ds(n, 16), :])[0:1]
        s += root_decode(rec[i, pl.ds(0, n), :], ex)
    top, z, t = stats[0:1, :], stats[1:2, :], stats[2:3, :]
    p = e[...] * jnp.exp(own[0:1, :] - top) / z
    target = s / t
    lg[...] = loss_scale * jnp.where(visible_mask(kp[...], qp[...]), p - target, 0.0)


def lg_call(rec, e, own, stats, kp, qp):
    return pl.pallas_call(
        lg_kernel,
        out_shape=jax.ShapeDtypeStruct(e.shape, f32),
        compiler_params=params(),
        cost_estimate=pl.CostEstimate(flops=8 * rec.size, bytes_accessed=2 * rec.size, transcendentals=0),
        name="logit_grad",
    )(rec, e, own, stats, kp, qp)


def grads_kernel(scale, half_rows, first, *refs):
    if first:
        keys, keys_t, lg_ref, q, out, gk = refs
    else:
        keys, keys_t, lg_ref, q, gk_in, out, gk = refs
    queries = lg_ref.shape[1]
    width = keys.shape[1]
    half = width // 2

    @pl.when(pl.program_id(0) == 0)
    def _():
        gk[...] = jnp.zeros(gk.shape, f32) if first else gk_in[...]

    k = keys[...]
    lg = lg_ref[...]
    w = q[0, pl.ds(half_rows, 16), :].astype(f32) * scale
    for pair in range(half_rows // queries // 2):
        qp = q[0, pl.ds(pair * 2 * queries, 2 * queries), :]
        s = dot(k, qp, NT)
        pres = []
        for u in range(2):
            row = pair * 2 + u
            su = s[:, u * queries : (u + 1) * queries]
            pres.append(jnp.where(su > 0.0, w[row : row + 1] * lg, 0.0).astype(bf16))
            gw = scale * jnp.sum(jnp.maximum(su, 0.0) * lg, axis=0, keepdims=True)
            for v in range(2):
                out[row * 2 + v, pl.ds(half, 8), :] = jnp.broadcast_to(gw, (8, queries))
        pre = jnp.concatenate(pres, axis=1)
        gk[...] += dot(pre, qp)
        gq = dot(keys_t[...], pre)
        for u in range(2):
            for v in range(2):
                out[(pair * 2 + u) * 2 + v, pl.ds(0, half), :] = gq[
                    v * half : (v + 1) * half, u * queries : (u + 1) * queries
                ]


def grads_call(keys, keys_t, lg, q, gk_in, scale, half_rows):
    n, width = keys.shape
    parts, rows, _ = q.shape
    queries = lg.shape[1]
    per = 2 * half_rows // queries
    full = lambda a: pl.BlockSpec(a.shape, lambda d: (0, 0))
    first = gk_in is None
    args = [keys, keys_t, lg, q] + ([] if first else [gk_in])
    specs = [full(keys), full(keys_t), full(lg), pl.BlockSpec((1, rows, width), lambda d: (d, 0, 0))]
    specs += [] if first else [full(gk_in)]
    return pl.pallas_call(
        functools.partial(grads_kernel, scale, half_rows, first),
        grid=(parts,),
        in_specs=specs,
        out_specs=[
            pl.BlockSpec((per, width // 2 + 8, queries), lambda d: (d, 0, 0)),
            pl.BlockSpec((n, width), lambda d: (0, 0)),
        ],
        out_shape=[
            jax.ShapeDtypeStruct((parts * per, width // 2 + 8, queries), f32),
            jax.ShapeDtypeStruct((n, width), f32),
        ],
        compiler_params=params(),
        cost_estimate=pl.CostEstimate(
            flops=3 * 2 * n * parts * half_rows * width,
            bytes_accessed=parts * rows * width * 6,
            transcendentals=0,
        ),
        name="grads",
    )(*args)


def code_kernel(a, b, out):
    x = a[...] + b[...]
    half = x.shape[1] - 8
    queries = x.shape[2]
    for i in range(x.shape[0]):
        g = x[i, 0:half]
        e = exponent(jnp.max(jnp.abs(g), axis=0, keepdims=True))
        out[i, pl.ds(0, half), :] = to_code(shrink(g, e) * 32767.0)
        w = x[i, half : half + 8]
        ew = exponent(jnp.abs(w))
        fine = shrink(w, ew) * 32767.0
        hi = jnp.floor(fine + 0.5)
        lo = (fine - hi) * 65534.0
        e16 = jnp.broadcast_to(e, (16, queries))
        spare = jnp.concatenate([ew, ew], axis=0)
        row = lax.broadcasted_iota(jnp.int32, (16, queries), 0)
        spare = jnp.where(row == 0, e16, spare)
        spare = jnp.where(row == 2, jnp.concatenate([hi, hi], axis=0), spare)
        spare = jnp.where(row == 3, jnp.concatenate([lo, lo], axis=0), spare)
        out[i, pl.ds(half, 16), :] = to_code(spare)


def code_call(a, b, parts):
    n, rows, queries = a.shape
    per = n // parts
    spec = pl.BlockSpec((per, rows, queries), lambda d: (d, 0, 0))
    return pl.pallas_call(
        code_kernel,
        grid=(parts,),
        in_specs=[spec, spec],
        out_specs=pl.BlockSpec((per, rows + 8, queries), lambda d: (d, 0, 0)),
        out_shape=jax.ShapeDtypeStruct((n, rows + 8, queries), jnp.int16),
        compiler_params=params(),
        name="code_parts",
    )(a, b)


def sum_kernel(rec, out):
    half = rec.shape[1] - 16
    queries = rec.shape[2]
    g = jnp.zeros((half, queries), f32)
    w = jnp.zeros((1, queries), f32)
    for i in range(rec.shape[0]):
        spare = from_code(rec[i, pl.ds(half, 16), :])
        g += grow(from_code(rec[i, pl.ds(0, half), :]) * (1.0 / 32767.0), spare[0:1])
        w += grow((spare[2:3] + spare[3:4] * (1.0 / 65534.0)) * (1.0 / 32767.0), spare[1:2])
    for i in range(out.shape[0]):
        out[i, pl.ds(0, half), :] = g
        out[i, pl.ds(half, 8), :] = jnp.broadcast_to(w, (8, queries))


def sum_call(rec, copies):
    n, rows, queries = rec.shape
    return pl.pallas_call(
        sum_kernel,
        out_shape=jax.ShapeDtypeStruct((copies, rows - 8, queries), f32),
        compiler_params=params(),
        name="sum_parts",
    )(rec)


def place_kernel(core, mine, other, gq, gw):
    heads, _, width = gq.shape
    half = width // 2
    for j in range(heads):
        side, jj = j // (heads // 2), j % (heads // 2)
        own = core[0] == side
        pick = lambda i: jnp.where(own, mine[i], other[i])
        lo, hi = pick(2 * jj), pick(2 * jj + 1)
        gq[j] = jnp.transpose(jnp.concatenate([lo[0:half], hi[0:half]], axis=0))
        gw[pl.ds(j, 1), :] = lo[half : half + 1]


def place_call(core, mine, other, heads, width):
    queries = mine.shape[2]
    vmem = pl.BlockSpec(memory_space=pltpu.VMEM)
    return pl.pallas_call(
        place_kernel,
        in_specs=[pl.BlockSpec(memory_space=pltpu.SMEM), vmem, vmem],
        out_specs=[vmem, vmem],
        out_shape=[
            jax.ShapeDtypeStruct((heads, queries, width), f32),
            jax.ShapeDtypeStruct((heads, queries), f32),
        ],
        compiler_params=params(),
        name="place",
    )(core.reshape(1), mine, other)


def merge(parts):
    top = functools.reduce(jnp.maximum, [p[0:1] for p in parts])
    z = sum(p[1:2] * jnp.exp(p[0:1] - top) for p in parts)
    t = sum(p[2:3] for p in parts)
    return jnp.concatenate([top, z, t, t], axis=0)


def ring_merge(s, axes):
    n = lax.axis_size(axes)
    moved = [lax.ppermute(s, axes, [(i, (i + k) % n) for i in range(n)]) for k in range(1, n)]
    return merge([s] + moved)


def spread(x, axes, count):
    return lax.all_to_all(jnp.broadcast_to(x[None], (count,) + x.shape), axes, 0, 0, tiled=True)


HEAD = ("zh", "x")
ZY = ("zl", "y")


def per_device(
    mla_queries,
    latent_cache,
    normalizers,
    query_positions,
    key_positions,
    index_queries,
    index_keys,
    index_weights,
):
    query_count = mla_queries.shape[1]
    sub_keys, index_width = index_keys.shape
    parts = lax.axis_size(HEAD)
    zy = lax.axis_size(ZY)
    local_heads = index_queries.shape[0]
    half_heads = local_heads // 2
    half_rows = half_heads * query_count
    index_scale = (local_heads * parts * index_width) ** (-0.5)
    core = lax.axis_index("core")
    swap = [(0, 1), (1, 0)]
    qp = query_positions.reshape(1, query_count)

    own_q = lax.dynamic_slice_in_dim(index_queries, core * half_heads, half_heads, 0)
    own_w = lax.dynamic_slice_in_dim(index_weights, core * half_heads, half_heads, 0)
    own = jnp.concatenate(
        [
            own_q.reshape(half_rows, index_width),
            jnp.pad(own_w, ((0, 16 - half_heads), (0, 0))),
        ],
        axis=0,
    )
    q_mine = spread(own, HEAD, parts)
    cache_t = latent_cache.T
    mla_t = mla_queries.transpose(0, 2, 1)
    probs = functools.partial(probs_call, cache_t, mla_t, normalizers, key_positions, qp, parts)
    coded, total_a = probs(0, parts // 2, None)
    q_mine, coded = lax.optimization_barrier((q_mine, coded))
    q_other = lax.ppermute(q_mine, "core", swap)

    offset = lax.axis_index(HEAD) * sub_keys
    own_kp = lax.dynamic_slice_in_dim(key_positions, offset, sub_keys, 0).reshape(1, sub_keys)
    acc = logits_call(index_keys, q_mine, None, own_kp, qp, index_scale, half_rows)
    e, local = logits_call(index_keys, q_other, acc, own_kp, qp, index_scale, half_rows)
    coded, e = lax.optimization_barrier((coded, e))
    coded, total_b = probs(parts // 2, parts // 2, coded)

    stats = jnp.concatenate([local[0:2], (total_a + total_b)[0:2]], axis=0)
    stats = ring_merge(stats, "core")
    stats, coded = lax.optimization_barrier((stats, coded))
    rec = lax.all_to_all(coded, HEAD, 0, 0, tiled=True)
    for axes in ("y", ("zh", "zl"), "x"):
        stats = ring_merge(stats, axes)
    lg = lg_call(rec, e, local, stats, own_kp, qp)

    keys_t = index_keys.T
    out_other, gk = grads_call(index_keys, keys_t, lg, q_other, None, index_scale, half_rows)
    got = lax.ppermute(out_other, "core", swap)
    out_mine, gk = grads_call(index_keys, keys_t, lg, q_mine, gk, index_scale, half_rows)
    block = lax.all_to_all(code_call(out_mine, got, parts), HEAD + ZY, 0, 0, tiled=True)
    mine = lax.all_to_all(sum_call(block, zy), ZY, 0, 0, tiled=True)
    other = lax.ppermute(mine, "core", swap)
    gq, gw = place_call(core, mine, other, local_heads, index_width)
    return gq, gw, gk


def solution(mesh):
    fine = Mesh(mesh.devices.reshape(2, 4, 2, 4, 2), HEAD + ZY + ("core",))
    ctx = ZY + ("core",)
    placed = (
        P(HEAD, None, None),
        P(ctx, None),
        P(HEAD, None),
        P(),
        P(ctx),
        P(HEAD, None, None),
        P(ctx + HEAD, None),
        P(HEAD, None),
    )
    return jax.shard_map(
        per_device,
        mesh=fine,
        in_specs=placed,
        out_specs=(P(HEAD, None, None), P(HEAD, None), P(ctx + HEAD, None)),
        check_vma=False,
    )
```

```python
import functools
import math

import jax
import jax.numpy as jnp
from jax import lax
from jax.experimental import pallas as pl
from jax.experimental.pallas import tpu as pltpu
from jax.sharding import Mesh
from jax.sharding import PartitionSpec as P

att_scale = 192.0 ** (-0.5)
loss_scale = 1024.0
masked_floor = -1e30
log2e = math.log2(math.e)
per_step = 4

NT = (((1,), (1,)), ((), ()))
NN = (((1,), (0,)), ((), ()))
f32 = jnp.float32
bf16 = jnp.bfloat16


def dot(a, b, dims=NN):
    return lax.dot_general(a, b, dims, preferred_element_type=f32)


def visible_mask(kp_row, qp_row):
    n = kp_row.shape[1]
    q = qp_row.shape[1]
    kp = jnp.transpose(jnp.broadcast_to(kp_row, (q, n)))
    return kp <= jnp.broadcast_to(qp_row, (n, q))


def params(mb=40):
    return pltpu.CompilerParams(vmem_limit_bytes=mb * 1024 * 1024)


def exponent(top):
    return jnp.clip(jnp.ceil(jnp.log2(jnp.maximum(top, 1e-37))), -122.0, 128.0)


def shrink(x, e):
    r = jnp.exp2(e * -0.5)
    return (x * r) * r


def grow(x, e):
    r = jnp.exp2(e * 0.5)
    return (x * r) * r


def to_code(x):
    return jnp.clip(jnp.floor(x + 0.5), -32768.0, 32767.0).astype(jnp.int32).astype(jnp.int16)


def from_code(c):
    return c.astype(jnp.int32).astype(f32)


def root_code(x, e):
    return to_code(jnp.sqrt(jnp.sqrt(shrink(x, e))) * 65535.0 - 32768.0)


def root_decode(c, e):
    r = (from_code(c) + 32768.0) * (1.0 / 65535.0) * jnp.exp2(e * 0.25)
    r = r * r
    return r * r


def probs_kernel(cache, q, nrm, kp, qp, out, tot):
    keys = cache.shape[1]
    heads, queries = nrm.shape

    @pl.when(pl.program_id(0) == 0)
    def _():
        tot[...] = jnp.zeros(tot.shape, f32)

    rows = keys // 2
    sums = []
    xt = jnp.transpose(cache[...])
    for block in range(2):
        x = xt[block * rows : (block + 1) * rows]
        acc = jnp.zeros((rows, queries), f32)
        for pair in range(heads // 2):
            s = dot(x, jnp.concatenate([q[pair * 2], q[pair * 2 + 1]], axis=1))
            for u in range(2):
                n = nrm[pl.ds(pair * 2 + u, 1), :] * log2e
                acc += jnp.exp2(s[:, u * queries : (u + 1) * queries] * (att_scale * log2e) - n)
        sums.append(acc)
    summed = jnp.concatenate(sums, axis=0)
    summed = jnp.where(visible_mask(kp[0], qp[...]), summed, 0.0)
    e = exponent(jnp.max(summed, axis=0, keepdims=True))
    out[0, pl.ds(0, keys), :] = root_code(summed, e)
    out[0, pl.ds(keys, 16), :] = to_code(jnp.broadcast_to(e, (16, queries)))
    tot[...] += jnp.broadcast_to(jnp.sum(summed, axis=0, keepdims=True), tot.shape)


def probs_call(cache_t, q_t, nrm, kp, qp, parts):
    width, keys = cache_t.shape
    rows = keys // parts
    heads, queries = nrm.shape
    return pl.pallas_call(
        probs_kernel,
        grid=(parts,),
        in_specs=[
            pl.BlockSpec((width, rows), lambda d: (0, d)),
            pl.BlockSpec(q_t.shape, lambda d: (0, 0, 0)),
            pl.BlockSpec(nrm.shape, lambda d: (0, 0)),
            pl.BlockSpec((1, 1, rows), lambda d: (d, 0, 0)),
            pl.BlockSpec(qp.shape, lambda d: (0, 0)),
        ],
        out_specs=[
            pl.BlockSpec((1, rows + 16, queries), lambda d: (d, 0, 0)),
            pl.BlockSpec((8, queries), lambda d: (0, 0)),
        ],
        out_shape=[
            jax.ShapeDtypeStruct((parts, rows + 16, queries), jnp.int16),
            jax.ShapeDtypeStruct((8, queries), f32),
        ],
        compiler_params=params(56),
        cost_estimate=pl.CostEstimate(
            flops=2 * keys * q_t.size,
            bytes_accessed=cache_t.size * 2 + q_t.size * 2,
            transcendentals=keys * heads * queries,
        ),
        name="probs",
    )(cache_t, q_t, nrm, kp.reshape(parts, 1, rows), qp)


def logits_kernel(scale, half_rows, first, *refs):
    if first:
        keys, q, acc = refs
    else:
        keys, q, before, kp, qp, e_out, stats, keys_t, acc = refs
    queries = acc.shape[1]
    step = pl.program_id(0)

    @pl.when(step == 0)
    def _():
        acc[...] = jnp.zeros(acc.shape, f32) if first else before[...]

    k = keys[...]
    total = acc[...]
    for part in range(q.shape[0]):
        w = q[part, pl.ds(half_rows, 16), :].astype(f32)
        for pair in range(half_rows // queries // 2):
            s = dot(k, q[part, pl.ds(pair * 2 * queries, 2 * queries), :], NT)
            for u in range(2):
                row = pair * 2 + u
                total += jnp.maximum(s[:, u * queries : (u + 1) * queries], 0.0) * w[row : row + 1]
    acc[...] = total
    if first:
        return

    @pl.when(step == pl.num_programs(0) - 1)
    def _():
        vis = visible_mask(kp[...], qp[...])
        hidden = jnp.where(vis, acc[...] * scale, masked_floor)
        m = jnp.max(hidden, axis=0, keepdims=True)
        e = jnp.where(vis, jnp.exp(hidden - m), 0.0)
        e_out[...] = e
        keys_t[...] = jnp.transpose(k)
        z = jnp.sum(e, axis=0, keepdims=True)
        rows = lax.broadcasted_iota(jnp.int32, stats.shape, 0)
        stats[...] = jnp.where(rows == 0, m, z)


def logits_call(keys, q, before, kp, qp, scale, half_rows):
    n, width = keys.shape
    parts, rows, _ = q.shape
    queries = qp.shape[1]
    full = lambda a: pl.BlockSpec(a.shape, lambda d: (0, 0))
    first = before is None
    whole = pl.BlockSpec((n, queries), lambda d: (0, 0))
    args = [keys, q] + ([] if first else [before, kp, qp])
    specs = [full(keys), pl.BlockSpec((per_step, rows, width), lambda d: (d, 0, 0))]
    specs += [] if first else [full(before), full(kp), full(qp)]
    table = jax.ShapeDtypeStruct((n, queries), f32)
    return pl.pallas_call(
        functools.partial(logits_kernel, scale, half_rows, first),
        grid=(parts // per_step,),
        in_specs=specs,
        out_specs=whole if first else [whole, pl.BlockSpec((8, queries), lambda d: (0, 0)), pl.BlockSpec((width, n), lambda d: (0, 0))],
        out_shape=table if first else [table, jax.ShapeDtypeStruct((8, queries), f32), jax.ShapeDtypeStruct((width, n), bf16)],
        scratch_shapes=[] if first else [pltpu.VMEM((n, queries), f32)],
        compiler_params=params(),
        cost_estimate=pl.CostEstimate(
            flops=2 * 2 * n * parts * half_rows * width,
            bytes_accessed=parts * rows * width * 2,
            transcendentals=0,
        ),
        name="logits",
    )(*args)


def lg_kernel(rec, e, own, stats, kp, qp, lg):
    n = e.shape[0]
    s = jnp.zeros(e.shape, f32)
    for i in range(rec.shape[0]):
        ex = from_code(rec[i, pl.ds(n, 16), :])[0:1]
        s += root_decode(rec[i, pl.ds(0, n), :], ex)
    m_all, z_all, t_all = stats[:, 0, :], stats[:, 1, :], stats[:, 2, :]
    top = jnp.max(m_all, axis=0, keepdims=True)
    z = jnp.sum(z_all * jnp.exp(m_all - top), axis=0, keepdims=True)
    t = jnp.sum(t_all, axis=0, keepdims=True)
    p = e[...] * jnp.exp(own[0:1, :] - top) / z
    target = s / t
    lg[...] = loss_scale * jnp.where(visible_mask(kp[...], qp[...]), p - target, 0.0)


def lg_call(rec, e, own, stats, kp, qp):
    return pl.pallas_call(
        lg_kernel,
        out_shape=jax.ShapeDtypeStruct(e.shape, f32),
        compiler_params=params(),
        cost_estimate=pl.CostEstimate(flops=8 * rec.size, bytes_accessed=2 * rec.size, transcendentals=0),
        name="logit_grad",
    )(rec, e, own, stats, kp, qp)


def grads_kernel(scale, half_rows, first, *refs):
    if first:
        keys, keys_t, lg_ref, q, out, gk = refs
    else:
        keys, keys_t, lg_ref, q, gk_in, out, gk = refs
    queries = lg_ref.shape[1]
    width = keys.shape[1]
    half = width // 2

    @pl.when(pl.program_id(0) == 0)
    def _():
        gk[...] = jnp.zeros(gk.shape, f32) if first else gk_in[...]

    k = keys[...]
    lg = lg_ref[...]
    heads = half_rows // queries
    for part in range(q.shape[0]):
        w = q[part, pl.ds(half_rows, 16), :].astype(f32) * scale
        qp = q[part, pl.ds(0, half_rows), :]
        s = dot(k, qp, NT)
        pres = []
        for u in range(heads):
            su = s[:, u * queries : (u + 1) * queries]
            pres.append(jnp.where(su > 0.0, w[u : u + 1] * lg, 0.0).astype(bf16))
            gw = scale * jnp.sum(jnp.maximum(su, 0.0) * lg, axis=0, keepdims=True)
            for v in range(2):
                out[(part * heads + u) * 2 + v, pl.ds(half, 8), :] = jnp.broadcast_to(gw, (8, queries))
        pre = jnp.concatenate(pres, axis=1)
        gk[...] += dot(pre, qp)
        gq = dot(keys_t[...], pre)
        for u in range(heads):
            for v in range(2):
                out[(part * heads + u) * 2 + v, pl.ds(0, half), :] = gq[
                    v * half : (v + 1) * half, u * queries : (u + 1) * queries
                ]


def grads_call(keys, keys_t, lg, q, gk_in, scale, half_rows):
    n, width = keys.shape
    parts, rows, _ = q.shape
    queries = lg.shape[1]
    per = 2 * half_rows // queries
    full = lambda a: pl.BlockSpec(a.shape, lambda d: (0, 0))
    first = gk_in is None
    args = [keys, keys_t, lg, q] + ([] if first else [gk_in])
    specs = [full(keys), full(keys_t), full(lg), pl.BlockSpec((per_step, rows, width), lambda d: (d, 0, 0))]
    specs += [] if first else [full(gk_in)]
    return pl.pallas_call(
        functools.partial(grads_kernel, scale, half_rows, first),
        grid=(parts // per_step,),
        in_specs=specs,
        out_specs=[
            pl.BlockSpec((per * per_step, width // 2 + 8, queries), lambda d: (d, 0, 0)),
            pl.BlockSpec((n, width), lambda d: (0, 0)),
        ],
        out_shape=[
            jax.ShapeDtypeStruct((parts * per, width // 2 + 8, queries), f32),
            jax.ShapeDtypeStruct((n, width), f32),
        ],
        compiler_params=params(),
        cost_estimate=pl.CostEstimate(
            flops=3 * 2 * n * parts * half_rows * width,
            bytes_accessed=parts * rows * width * 6,
            transcendentals=0,
        ),
        name="grads",
    )(*args)


def code_kernel(a, b, out):
    x = a[...] + b[...]
    half = x.shape[1] - 8
    queries = x.shape[2]
    for i in range(x.shape[0]):
        g = x[i, 0:half]
        e = exponent(jnp.max(jnp.abs(g), axis=0, keepdims=True))
        out[i, pl.ds(0, half), :] = to_code(shrink(g, e) * 32767.0)
        w = x[i, half : half + 8]
        ew = exponent(jnp.abs(w))
        fine = shrink(w, ew) * 32767.0
        hi = jnp.floor(fine + 0.5)
        lo = (fine - hi) * 65534.0
        e16 = jnp.broadcast_to(e, (16, queries))
        spare = jnp.concatenate([ew, ew], axis=0)
        row = lax.broadcasted_iota(jnp.int32, (16, queries), 0)
        spare = jnp.where(row == 0, e16, spare)
        spare = jnp.where(row == 2, jnp.concatenate([hi, hi], axis=0), spare)
        spare = jnp.where(row == 3, jnp.concatenate([lo, lo], axis=0), spare)
        out[i, pl.ds(half, 16), :] = to_code(spare)


def code_call(a, b, parts):
    n, rows, queries = a.shape
    per = n // parts
    spec = pl.BlockSpec((per, rows, queries), lambda d: (d, 0, 0))
    return pl.pallas_call(
        code_kernel,
        grid=(parts,),
        in_specs=[spec, spec],
        out_specs=pl.BlockSpec((per, rows + 8, queries), lambda d: (d, 0, 0)),
        out_shape=jax.ShapeDtypeStruct((n, rows + 8, queries), jnp.int16),
        compiler_params=params(),
        name="code_parts",
    )(a, b)


def sum_kernel(rec, out):
    half = rec.shape[1] - 16
    queries = rec.shape[2]
    g = jnp.zeros((half, queries), f32)
    w = jnp.zeros((1, queries), f32)
    for i in range(rec.shape[0]):
        spare = from_code(rec[i, pl.ds(half, 16), :])
        g += grow(from_code(rec[i, pl.ds(0, half), :]) * (1.0 / 32767.0), spare[0:1])
        w += grow((spare[2:3] + spare[3:4] * (1.0 / 65534.0)) * (1.0 / 32767.0), spare[1:2])
    for i in range(out.shape[0]):
        out[i, pl.ds(0, half), :] = g
        out[i, pl.ds(half, 8), :] = jnp.broadcast_to(w, (8, queries))


def sum_call(rec, copies):
    n, rows, queries = rec.shape
    return pl.pallas_call(
        sum_kernel,
        out_shape=jax.ShapeDtypeStruct((copies, rows - 8, queries), f32),
        compiler_params=params(),
        name="sum_parts",
    )(rec)


def place_kernel(core, mine, other, gq, gw):
    heads, _, width = gq.shape
    half = width // 2
    for j in range(heads):
        side, jj = j // (heads // 2), j % (heads // 2)
        own = core[0] == side
        pick = lambda i: jnp.where(own, mine[i], other[i])
        lo, hi = pick(2 * jj), pick(2 * jj + 1)
        gq[j] = jnp.transpose(jnp.concatenate([lo[0:half], hi[0:half]], axis=0))
        gw[pl.ds(j, 1), :] = lo[half : half + 1]


def place_call(core, mine, other, heads, width):
    queries = mine.shape[2]
    vmem = pl.BlockSpec(memory_space=pltpu.VMEM)
    return pl.pallas_call(
        place_kernel,
        in_specs=[pl.BlockSpec(memory_space=pltpu.SMEM), vmem, vmem],
        out_specs=[vmem, vmem],
        out_shape=[
            jax.ShapeDtypeStruct((heads, queries, width), f32),
            jax.ShapeDtypeStruct((heads, queries), f32),
        ],
        compiler_params=params(),
        name="place",
    )(core.reshape(1), mine, other)


def spread(x, axes, count):
    return lax.all_to_all(jnp.broadcast_to(x[None], (count,) + x.shape), axes, 0, 0, tiled=True)


HEAD = ("zh", "x")
ZY = ("zl", "y")
CORE = ("core",)


def per_device(
    mla_queries,
    latent_cache,
    normalizers,
    query_positions,
    key_positions,
    index_queries,
    index_keys,
    index_weights,
):
    query_count = mla_queries.shape[1]
    sub_keys, index_width = index_keys.shape
    parts = lax.axis_size(HEAD)
    zy = lax.axis_size(ZY)
    local_heads = index_queries.shape[0]
    half_heads = local_heads // 2
    half_rows = half_heads * query_count
    index_scale = (local_heads * parts * index_width) ** (-0.5)
    core = lax.axis_index("core")
    swap = [(0, 1), (1, 0)]
    qp = query_positions.reshape(1, query_count)

    own_q = lax.dynamic_slice_in_dim(index_queries, core * half_heads, half_heads, 0)
    own_w = lax.dynamic_slice_in_dim(index_weights, core * half_heads, half_heads, 0)
    own = jnp.concatenate(
        [
            own_q.reshape(half_rows, index_width),
            jnp.pad(own_w, ((0, 16 - half_heads), (0, 0))),
        ],
        axis=0,
    )
    q_mine = spread(own, HEAD, parts)
    coded, total = probs_call(
        latent_cache.T, mla_queries.transpose(0, 2, 1), normalizers, key_positions, qp, parts
    )
    q_mine, coded = lax.optimization_barrier((q_mine, coded))
    q_other = lax.ppermute(q_mine, "core", swap)
    rec = lax.all_to_all(coded, HEAD, 0, 0, tiled=True)

    offset = lax.axis_index(HEAD) * sub_keys
    own_kp = lax.dynamic_slice_in_dim(key_positions, offset, sub_keys, 0).reshape(1, sub_keys)
    acc = logits_call(index_keys, q_mine, None, own_kp, qp, index_scale, half_rows)
    e, local, keys_t = logits_call(index_keys, q_other, acc, own_kp, qp, index_scale, half_rows)
    stats = jnp.concatenate([local[0:2], total[0:2]], axis=0)
    stats, rec = lax.optimization_barrier((stats, rec))
    stats = spread(stats, HEAD + ZY + CORE, parts * zy * 2)
    lg = lg_call(rec, e, local, stats, own_kp, qp)

    out_other, gk = grads_call(index_keys, keys_t, lg, q_other, None, index_scale, half_rows)
    got = lax.ppermute(out_other, "core", swap)
    out_mine, gk = grads_call(index_keys, keys_t, lg, q_mine, gk, index_scale, half_rows)
    block = lax.all_to_all(code_call(out_mine, got, parts), HEAD + ZY, 0, 0, tiled=True)
    mine = lax.all_to_all(sum_call(block, zy), ZY, 0, 0, tiled=True)
    other = lax.ppermute(mine, "core", swap)
    gq, gw = place_call(core, mine, other, local_heads, index_width)
    return gq, gw, gk


def solution(mesh):
    fine = Mesh(mesh.devices.reshape(2, 4, 2, 4, 2), HEAD + ZY + ("core",))
    ctx = ZY + ("core",)
    placed = (
        P(HEAD, None, None),
        P(ctx, None),
        P(HEAD, None),
        P(),
        P(ctx),
        P(HEAD, None, None),
        P(ctx + HEAD, None),
        P(HEAD, None),
    )
    return jax.shard_map(
        per_device,
        mesh=fine,
        in_specs=placed,
        out_specs=(P(HEAD, None, None), P(HEAD, None), P(ctx + HEAD, None)),
        check_vma=False,
    )
```

```python
import functools
import math

import jax
import jax.numpy as jnp
from jax import lax
from jax.experimental import pallas as pl
from jax.experimental.pallas import tpu as pltpu
from jax.sharding import Mesh
from jax.sharding import PartitionSpec as P

att_scale = 192.0 ** (-0.5)
loss_scale = 1024.0
masked_floor = -1e30
log2e = math.log2(math.e)
per_step = 4
grads_step = 4

NT = (((1,), (1,)), ((), ()))
NN = (((1,), (0,)), ((), ()))
f32 = jnp.float32
bf16 = jnp.bfloat16


def dot(a, b, dims=NN):
    return lax.dot_general(a, b, dims, preferred_element_type=f32)


def visible_mask(kp_row, qp_row):
    n = kp_row.shape[1]
    q = qp_row.shape[1]
    kp = jnp.transpose(jnp.broadcast_to(kp_row, (q, n)))
    return kp <= jnp.broadcast_to(qp_row, (n, q))


def params(mb=20):
    return pltpu.CompilerParams(vmem_limit_bytes=mb * 1024 * 1024)


def exponent(top):
    return jnp.clip(jnp.ceil(jnp.log2(jnp.maximum(top, 1e-37))), -122.0, 128.0)


def shrink(x, e):
    r = jnp.exp2(e * -0.5)
    return (x * r) * r


def grow(x, e):
    r = jnp.exp2(e * 0.5)
    return (x * r) * r


def to_code(x):
    return jnp.clip(jnp.floor(x + 0.5), -32768.0, 32767.0).astype(jnp.int32).astype(jnp.int16)


def from_code(c):
    return c.astype(jnp.int32).astype(f32)


def root_code(x, e):
    root = jnp.where(x > 0.0, lax.rsqrt(lax.rsqrt(x)), 0.0)
    return ((root * (65535.0 * jnp.exp2(e * -0.25)) + 0.5).astype(jnp.int32) - 32768).astype(jnp.int16)


def root_decode(c, e):
    r = (from_code(c) + 32768.0) * (1.0 / 65535.0) * jnp.exp2(e * 0.25)
    r = r * r
    return r * r


def probs_kernel(cache, q, nrm, kp, qp, out, tot):
    keys = cache.shape[1]
    heads, queries = nrm.shape

    @pl.when(pl.program_id(0) == 0)
    def _():
        tot[...] = jnp.zeros(tot.shape, f32)

    rows = keys // 2
    sums = []
    xt = jnp.transpose(cache[...])
    for block in range(2):
        x = xt[block * rows : (block + 1) * rows]
        acc = jnp.zeros((rows, queries), f32)
        for pair in range(heads // 2):
            s = dot(x, jnp.concatenate([q[pair * 2], q[pair * 2 + 1]], axis=1))
            for u in range(2):
                n = nrm[pl.ds(pair * 2 + u, 1), :] * log2e
                acc += jnp.exp2(s[:, u * queries : (u + 1) * queries] * (att_scale * log2e) - n)
        sums.append(acc)
    summed = jnp.concatenate(sums, axis=0)
    summed = jnp.where(visible_mask(kp[0], qp[...]), summed, 0.0)
    e = exponent(jnp.max(summed, axis=0, keepdims=True))
    out[0, pl.ds(0, keys), :] = root_code(summed, e)
    out[0, pl.ds(keys, 16), :] = to_code(jnp.broadcast_to(e, (16, queries)))
    tot[...] += jnp.broadcast_to(jnp.sum(summed, axis=0, keepdims=True), tot.shape)


def probs_call(cache_t, q_t, nrm, kp, qp, parts):
    width, keys = cache_t.shape
    rows = keys // parts
    heads, queries = nrm.shape
    return pl.pallas_call(
        probs_kernel,
        grid=(parts,),
        in_specs=[
            pl.BlockSpec((width, rows), lambda d: (0, d)),
            pl.BlockSpec(q_t.shape, lambda d: (0, 0, 0)),
            pl.BlockSpec(nrm.shape, lambda d: (0, 0)),
            pl.BlockSpec((1, 1, rows), lambda d: (d, 0, 0)),
            pl.BlockSpec(qp.shape, lambda d: (0, 0)),
        ],
        out_specs=[
            pl.BlockSpec((1, rows + 16, queries), lambda d: (d, 0, 0)),
            pl.BlockSpec((8, queries), lambda d: (0, 0)),
        ],
        out_shape=[
            jax.ShapeDtypeStruct((parts, rows + 16, queries), jnp.int16),
            jax.ShapeDtypeStruct((8, queries), f32),
        ],
        compiler_params=params(56),
        cost_estimate=pl.CostEstimate(
            flops=2 * keys * q_t.size,
            bytes_accessed=cache_t.size * 2 + q_t.size * 2,
            transcendentals=keys * heads * queries,
        ),
        name="probs",
    )(cache_t, q_t, nrm, kp.reshape(parts, 1, rows), qp)


def logits_kernel(scale, half_rows, first, *refs):
    if first:
        keys, q, acc = refs
    else:
        keys, q, before, kp, qp, e_out, stats, acc = refs
    queries = acc.shape[1]
    step = pl.program_id(0)

    @pl.when(step == 0)
    def _():
        acc[...] = jnp.zeros(acc.shape, f32) if first else before[...]

    k = keys[...]
    total = acc[...]
    for part in range(q.shape[0]):
        w = q[part, pl.ds(half_rows, 16), :].astype(f32)
        for pair in range(half_rows // queries // 2):
            s = dot(k, q[part, pl.ds(pair * 2 * queries, 2 * queries), :], NT)
            for u in range(2):
                row = pair * 2 + u
                total += jnp.maximum(s[:, u * queries : (u + 1) * queries], 0.0) * w[row : row + 1]
    acc[...] = total
    if first:
        return

    @pl.when(step == pl.num_programs(0) - 1)
    def _():
        vis = visible_mask(kp[...], qp[...])
        hidden = jnp.where(vis, acc[...] * scale, masked_floor)
        m = jnp.max(hidden, axis=0, keepdims=True)
        e = jnp.where(vis, jnp.exp(hidden - m), 0.0)
        e_out[...] = e
        z = jnp.sum(e, axis=0, keepdims=True)
        rows = lax.broadcasted_iota(jnp.int32, stats.shape, 0)
        stats[...] = jnp.where(rows == 0, m, z)


def logits_call(keys, q, before, kp, qp, scale, half_rows):
    n, width = keys.shape
    parts, rows, _ = q.shape
    queries = qp.shape[1]
    full = lambda a: pl.BlockSpec(a.shape, lambda d: (0, 0))
    first = before is None
    whole = pl.BlockSpec((n, queries), lambda d: (0, 0))
    args = [keys, q] + ([] if first else [before, kp, qp])
    specs = [full(keys), pl.BlockSpec((per_step, rows, width), lambda d: (d, 0, 0))]
    specs += [] if first else [full(before), full(kp), full(qp)]
    table = jax.ShapeDtypeStruct((n, queries), f32)
    return pl.pallas_call(
        functools.partial(logits_kernel, scale, half_rows, first),
        grid=(parts // per_step,),
        in_specs=specs,
        out_specs=whole if first else [whole, pl.BlockSpec((8, queries), lambda d: (0, 0))],
        out_shape=table if first else [table, jax.ShapeDtypeStruct((8, queries), f32)],
        scratch_shapes=[] if first else [pltpu.VMEM((n, queries), f32)],
        compiler_params=params(),
        cost_estimate=pl.CostEstimate(
            flops=2 * 2 * n * parts * half_rows * width,
            bytes_accessed=parts * rows * width * 2,
            transcendentals=0,
        ),
        name="logits",
    )(*args)


def lg_kernel(rec, e, own, stats, kp, qp, lg):
    n = e.shape[0]
    s = jnp.zeros(e.shape, f32)
    for i in range(rec.shape[0]):
        ex = from_code(rec[i, pl.ds(n, 16), :])[0:1]
        s += root_decode(rec[i, pl.ds(0, n), :], ex)
    every, queries = stats[:, 0, :], e.shape[1]
    m_all, z_all, t_all = (every[:, i * queries : (i + 1) * queries] for i in range(3))
    top = jnp.max(m_all, axis=0, keepdims=True)
    z = jnp.sum(z_all * jnp.exp(m_all - top), axis=0, keepdims=True)
    t = jnp.sum(t_all, axis=0, keepdims=True)
    p = e[...] * jnp.exp(own[0:1, :] - top) / z
    target = s / t
    lg[...] = loss_scale * jnp.where(visible_mask(kp[...], qp[...]), p - target, 0.0)


def lg_call(rec, e, own, stats, kp, qp):
    return pl.pallas_call(
        lg_kernel,
        out_shape=jax.ShapeDtypeStruct(e.shape, f32),
        compiler_params=params(),
        cost_estimate=pl.CostEstimate(flops=8 * rec.size, bytes_accessed=2 * rec.size, transcendentals=0),
        name="logit_grad",
    )(rec, e, own, stats, kp, qp)


def grads_kernel(scale, half_rows, sides, sums, more, gk_out, gk_more, which, keys, lg_ref, *refs):
    refs = list(refs)
    take = lambda count: [refs.pop(0) for _ in range(count)]
    qs = take(sides)
    befores = take(sides if more else 0)
    gk_in = take(1)[0] if gk_more else None
    outs = take(sides if sums else 0)
    gk = take(1)[0] if gk_out else None
    keys_t = take(1)[0]
    queries = lg_ref.shape[1]
    width = keys.shape[1]
    half = width // 2

    @pl.when(pl.program_id(0) == 0)
    def _():
        if gk_out:
            gk[...] = gk_in[...] if gk_more else jnp.zeros(gk.shape, f32)
        keys_t[...] = jnp.transpose(keys[...])

    k = keys[...]
    lg = lg_ref[...]
    heads = half_rows // queries
    for side in range(sides):
        q = qs[side]
        for part in range(q.shape[1]):
            w = q[0, part, pl.ds(half_rows, 16), :].astype(f32) * scale
            qp = q[0, part, pl.ds(0, half_rows), :]
            s = dot(k, qp, NT)
            cut = lambda x, u: x[:, u * queries : (u + 1) * queries]
            pres = [
                jnp.where(cut(s, u) > 0.0, w[u : u + 1] * lg, 0.0).astype(bf16) for u in range(heads)
            ]
            pre = jnp.concatenate(pres, axis=1)
            if gk_out:
                gk[...] += dot(pre, qp)
            if not sums:
                continue
            gq = dot(keys_t[...], pre)
            for u in range(heads):
                gw = scale * jnp.sum(jnp.maximum(cut(s, u), 0.0) * lg, axis=0, keepdims=True)
                for v in range(2):
                    at = (part * heads + u) * 2 + v
                    block = cut(gq, u)[v * half : (v + 1) * half]
                    row = jnp.broadcast_to(gw, (8, queries))
                    if more:
                        block += befores[side][at, pl.ds(0, half), :]
                        row += befores[side][at, pl.ds(half, 8), :]
                    outs[side][at, pl.ds(0, half), :] = block
                    outs[side][at, pl.ds(half, 8), :] = row


def grads_call(which, keys, lg, qs, befores, gk_out, gk_in, scale, half_rows, sums=True):
    n, width = keys.shape
    parts, rows, _ = qs[0].shape
    queries = lg.shape[1]
    blocks = 2 * half_rows // queries * grads_step
    steps = parts // 2 // grads_step
    full = lambda a: pl.BlockSpec(a.shape, lambda d, z: (0, 0))
    part = pl.BlockSpec((1, grads_step, rows, width), lambda d, z: (z[0], d, 0, 0))
    out = pl.BlockSpec((blocks, width // 2 + 8, queries), lambda d, z: (d, 0, 0))
    more, gk_more = befores is not None, gk_in is not None
    args = [keys, lg] + [q.reshape(2, parts // 2, rows, width) for q in qs]
    args += (befores if more else []) + ([gk_in] if gk_more else [])
    specs = [full(keys), full(lg)] + [part] * len(qs)
    specs += [out] * len(qs) if more else []
    specs += [full(gk_in)] if gk_more else []
    table = jax.ShapeDtypeStruct((steps * blocks, width // 2 + 8, queries), f32)
    given = len(qs) if sums else 0
    return pl.pallas_call(
        functools.partial(grads_kernel, scale, half_rows, len(qs), sums, more, gk_out, gk_more),
        grid_spec=pltpu.PrefetchScalarGridSpec(
            num_scalar_prefetch=1,
            grid=(steps,),
            in_specs=specs,
            out_specs=[out] * given + [pl.BlockSpec((n, width), lambda d, z: (0, 0))] * gk_out,
            scratch_shapes=[pltpu.VMEM((width, n), bf16)],
        ),
        out_shape=[table] * given + [jax.ShapeDtypeStruct((n, width), f32)] * gk_out,
        compiler_params=params(),
        cost_estimate=pl.CostEstimate(
            flops=3 * n * parts * len(qs) * half_rows * width,
            bytes_accessed=parts * len(qs) * rows * width * 3,
            transcendentals=0,
        ),
        name="grads",
    )(which, *args)


def code_kernel(a, b, out):
    x = a[...] + b[...]
    half = x.shape[1] - 8
    queries = x.shape[2]
    for i in range(x.shape[0]):
        g = x[i, 0:half]
        e = exponent(jnp.max(jnp.abs(g), axis=0, keepdims=True))
        out[i, pl.ds(0, half), :] = to_code(shrink(g, e) * 32767.0)
        w = x[i, half : half + 8]
        ew = exponent(jnp.abs(w))
        fine = shrink(w, ew) * 32767.0
        hi = jnp.floor(fine + 0.5)
        lo = (fine - hi) * 65534.0
        e16 = jnp.broadcast_to(e, (16, queries))
        spare = jnp.concatenate([ew, ew], axis=0)
        row = lax.broadcasted_iota(jnp.int32, (16, queries), 0)
        spare = jnp.where(row == 0, e16, spare)
        spare = jnp.where(row == 2, jnp.concatenate([hi, hi], axis=0), spare)
        spare = jnp.where(row == 3, jnp.concatenate([lo, lo], axis=0), spare)
        out[i, pl.ds(half, 16), :] = to_code(spare)


def code_call(a, b, parts):
    n, rows, queries = a.shape
    per = n // parts
    spec = pl.BlockSpec((per, rows, queries), lambda d: (d, 0, 0))
    return pl.pallas_call(
        code_kernel,
        grid=(parts,),
        in_specs=[spec, spec],
        out_specs=pl.BlockSpec((per, rows + 8, queries), lambda d: (d, 0, 0)),
        out_shape=jax.ShapeDtypeStruct((n, rows + 8, queries), jnp.int16),
        compiler_params=params(),
        name="code_parts",
    )(a, b)


def sum_kernel(rec, out):
    half = rec.shape[1] - 16
    queries = rec.shape[2]
    g = jnp.zeros((half, queries), f32)
    w = jnp.zeros((1, queries), f32)
    for i in range(rec.shape[0]):
        spare = from_code(rec[i, pl.ds(half, 16), :])
        g += grow(from_code(rec[i, pl.ds(0, half), :]) * (1.0 / 32767.0), spare[0:1])
        w += grow((spare[2:3] + spare[3:4] * (1.0 / 65534.0)) * (1.0 / 32767.0), spare[1:2])
    for i in range(out.shape[0]):
        out[i, pl.ds(0, half), :] = g
        out[i, pl.ds(half, 8), :] = jnp.broadcast_to(w, (8, queries))


def sum_call(rec, copies):
    n, rows, queries = rec.shape
    return pl.pallas_call(
        sum_kernel,
        out_shape=jax.ShapeDtypeStruct((copies, rows - 8, queries), f32),
        compiler_params=params(),
        name="sum_parts",
    )(rec)


def place_kernel(core, mine, other, gq, gw):
    heads, _, width = gq.shape
    half = width // 2
    for j in range(heads):
        side, jj = j // (heads // 2), j % (heads // 2)
        own = core[0] == side
        pick = lambda i: jnp.where(own, mine[i], other[i])
        lo, hi = pick(2 * jj), pick(2 * jj + 1)
        gq[j] = jnp.transpose(jnp.concatenate([lo[0:half], hi[0:half]], axis=0))
        gw[pl.ds(j, 1), :] = lo[half : half + 1]


def place_call(core, mine, other, heads, width):
    queries = mine.shape[2]
    vmem = pl.BlockSpec(memory_space=pltpu.VMEM)
    return pl.pallas_call(
        place_kernel,
        in_specs=[pl.BlockSpec(memory_space=pltpu.SMEM), vmem, vmem],
        out_specs=[vmem, vmem],
        out_shape=[
            jax.ShapeDtypeStruct((heads, queries, width), f32),
            jax.ShapeDtypeStruct((heads, queries), f32),
        ],
        compiler_params=params(),
        name="place",
    )(core.reshape(1), mine, other)


def spread(x, axes, count):
    return lax.all_to_all(jnp.broadcast_to(x[None], (count,) + x.shape), axes, 0, 0, tiled=True)


HEAD = ("zh", "x")
ZY = ("zl", "y")
CORE = ("core",)


def per_device(
    mla_queries,
    latent_cache,
    normalizers,
    query_positions,
    key_positions,
    index_queries,
    index_keys,
    index_weights,
):
    query_count = mla_queries.shape[1]
    sub_keys, index_width = index_keys.shape
    parts = lax.axis_size(HEAD)
    zy = lax.axis_size(ZY)
    local_heads = index_queries.shape[0]
    half_heads = local_heads // 2
    half_rows = half_heads * query_count
    index_scale = (local_heads * parts * index_width) ** (-0.5)
    core = lax.axis_index("core")
    swap = [(0, 1), (1, 0)]
    qp = query_positions.reshape(1, query_count)

    own_q = lax.dynamic_slice_in_dim(index_queries, core * half_heads, half_heads, 0)
    own_w = lax.dynamic_slice_in_dim(index_weights, core * half_heads, half_heads, 0)
    own = jnp.concatenate(
        [
            own_q.reshape(half_rows, index_width),
            jnp.pad(own_w, ((0, 16 - half_heads), (0, 0))),
        ],
        axis=0,
    )
    q_mine = spread(own, HEAD, parts)
    coded, total = probs_call(
        latent_cache.T, mla_queries.transpose(0, 2, 1), normalizers, key_positions, qp, parts
    )
    pair_keys = lax.ppermute(index_keys, "zh", swap)
    q_mine, coded, pair_keys = lax.optimization_barrier((q_mine, coded, pair_keys))
    q_other = lax.ppermute(q_mine, "core", swap)
    rec = lax.all_to_all(coded, HEAD, 0, 0, tiled=True)

    offset = lax.axis_index(HEAD) * sub_keys
    own_kp = lax.dynamic_slice_in_dim(key_positions, offset, sub_keys, 0).reshape(1, sub_keys)
    acc = logits_call(index_keys, q_mine, None, own_kp, qp, index_scale, half_rows)
    e, local = logits_call(index_keys, q_other, acc, own_kp, qp, index_scale, half_rows)
    stats = jnp.concatenate([local[0:1], local[1:2], total[0:1]], axis=1)
    side = lax.axis_index("zh").reshape(1)
    stats, rec, side, far = lax.optimization_barrier((stats, rec, side, 1 - side))
    stats = spread(stats, HEAD + ZY + CORE, parts * zy * 2)
    lg = lg_call(rec, e, local, stats, own_kp, qp)

    pair_lg = lax.ppermute(lg, "zh", swap)
    grads = functools.partial(grads_call, scale=index_scale, half_rows=half_rows)
    own_other, own_mine, gk = grads(side, index_keys, lg, [q_other, q_mine], None, True, None)
    (gk,) = grads(far, index_keys, lg, [q_other, q_mine], None, True, gk, sums=False)
    (own_other, own_mine, gk, pair_lg) = lax.optimization_barrier((own_other, own_mine, gk, pair_lg))
    (out_other,) = grads(side, pair_keys, pair_lg, [q_other], [own_other], False, None)
    got = lax.ppermute(out_other, "core", swap)
    (out_mine,) = grads(side, pair_keys, pair_lg, [q_mine], [own_mine], False, None)
    block = lax.all_to_all(code_call(out_mine, got, parts // 2), ("x",) + ZY, 0, 0, tiled=True)
    mine = lax.all_to_all(sum_call(block, zy), ZY, 0, 0, tiled=True)
    other = lax.ppermute(mine, "core", swap)
    gq, gw = place_call(core, mine, other, local_heads, index_width)
    return gq, gw, gk


def solution(mesh):
    fine = Mesh(mesh.devices.reshape(2, 4, 2, 4, 2), HEAD + ZY + ("core",))
    ctx = ZY + ("core",)
    placed = (
        P(HEAD, None, None),
        P(ctx, None),
        P(HEAD, None),
        P(),
        P(ctx),
        P(HEAD, None, None),
        P(ctx + HEAD, None),
        P(HEAD, None),
    )
    return jax.shard_map(
        per_device,
        mesh=fine,
        in_specs=placed,
        out_specs=(P(HEAD, None, None), P(HEAD, None), P(ctx + HEAD, None)),
        check_vma=False,
    )
```

```python
import functools
import math

import jax
import jax.numpy as jnp
from jax import lax
from jax.experimental import pallas as pl
from jax.experimental.pallas import tpu as pltpu
from jax.sharding import Mesh
from jax.sharding import PartitionSpec as P

att_scale = 192.0 ** (-0.5)
loss_scale = 1024.0
masked_floor = -1e30
log2e = math.log2(math.e)
per_step = 4
grads_step = 4
row_blocks = 4

NT = (((1,), (1,)), ((), ()))
NN = (((1,), (0,)), ((), ()))
f32 = jnp.float32
bf16 = jnp.bfloat16


def dot(a, b, dims=NN):
    return lax.dot_general(a, b, dims, preferred_element_type=f32)


def visible_mask(kp_row, qp_row):
    n = kp_row.shape[1]
    q = qp_row.shape[1]
    kp = jnp.transpose(jnp.broadcast_to(kp_row, (q, n)))
    return kp <= jnp.broadcast_to(qp_row, (n, q))


def params(mb=20):
    return pltpu.CompilerParams(vmem_limit_bytes=mb * 1024 * 1024)


def exponent(top):
    return jnp.clip(jnp.ceil(jnp.log2(jnp.maximum(top, 1e-37))), -122.0, 128.0)


def shrink(x, e):
    r = jnp.exp2(e * -0.5)
    return (x * r) * r


def grow(x, e):
    r = jnp.exp2(e * 0.5)
    return (x * r) * r


def to_code(x):
    return jnp.clip(jnp.floor(x + 0.5), -32768.0, 32767.0).astype(jnp.int32).astype(jnp.int16)


def from_code(c):
    return c.astype(jnp.int32).astype(f32)


def root_code(x, e):
    root = jnp.where(x > 0.0, lax.rsqrt(lax.rsqrt(x)), 0.0)
    return ((root * (65535.0 * jnp.exp2(e * -0.25)) + 0.5).astype(jnp.int32) - 32768).astype(jnp.int16)


def root_decode(c, e):
    r = (from_code(c) + 32768.0) * (1.0 / 65535.0) * jnp.exp2(e * 0.25)
    r = r * r
    return r * r


def probs_kernel(cache, q, nrm, kp, qp, out, tot):
    keys = cache.shape[1]
    heads, queries = nrm.shape

    @pl.when(pl.program_id(0) == 0)
    def _():
        tot[...] = jnp.zeros(tot.shape, f32)

    rows = keys // row_blocks
    xt = jnp.transpose(cache[...])
    e_rows = []
    total = jnp.zeros((1, queries), f32)
    for block in range(row_blocks):
        x = xt[block * rows : (block + 1) * rows]
        acc = jnp.zeros((rows, queries), f32)
        for pair in range(heads // 2):
            s = dot(x, jnp.concatenate([q[pair * 2], q[pair * 2 + 1]], axis=1))
            for u in range(2):
                n = nrm[pl.ds(pair * 2 + u, 1), :] * log2e
                acc += jnp.exp2(s[:, u * queries : (u + 1) * queries] * (att_scale * log2e) - n)
        acc = jnp.where(visible_mask(kp[0, :, pl.ds(block * rows, rows)], qp[...]), acc, 0.0)
        e = exponent(jnp.max(acc, axis=0, keepdims=True))
        out[0, pl.ds(block * rows, rows), :] = root_code(acc, e)
        e_rows.append(jnp.broadcast_to(e, (16 // row_blocks, queries)))
        total += jnp.sum(acc, axis=0, keepdims=True)
    out[0, pl.ds(keys, 16), :] = to_code(jnp.concatenate(e_rows, axis=0))
    tot[...] += jnp.broadcast_to(total, tot.shape)


def probs_call(cache_t, q_t, nrm, kp, qp, parts):
    width, keys = cache_t.shape
    rows = keys // parts
    heads, queries = nrm.shape
    return pl.pallas_call(
        probs_kernel,
        grid=(parts,),
        in_specs=[
            pl.BlockSpec((width, rows), lambda d: (0, d)),
            pl.BlockSpec(q_t.shape, lambda d: (0, 0, 0)),
            pl.BlockSpec(nrm.shape, lambda d: (0, 0)),
            pl.BlockSpec((1, 1, rows), lambda d: (d, 0, 0)),
            pl.BlockSpec(qp.shape, lambda d: (0, 0)),
        ],
        out_specs=[
            pl.BlockSpec((1, rows + 16, queries), lambda d: (d, 0, 0)),
            pl.BlockSpec((8, queries), lambda d: (0, 0)),
        ],
        out_shape=[
            jax.ShapeDtypeStruct((parts, rows + 16, queries), jnp.int16),
            jax.ShapeDtypeStruct((8, queries), f32),
        ],
        compiler_params=params(56),
        cost_estimate=pl.CostEstimate(
            flops=2 * keys * q_t.size,
            bytes_accessed=cache_t.size * 2 + q_t.size * 2,
            transcendentals=keys * heads * queries,
        ),
        name="probs",
    )(cache_t, q_t, nrm, kp.reshape(parts, 1, rows), qp)


def logits_kernel(scale, half_rows, first, *refs):
    if first:
        keys, q, acc = refs
    else:
        keys, q, before, kp, qp, e_out, stats, acc = refs
    queries = acc.shape[1]
    step = pl.program_id(0)

    @pl.when(step == 0)
    def _():
        acc[...] = jnp.zeros(acc.shape, f32) if first else before[...]

    k = keys[...]
    total = acc[...]
    for part in range(q.shape[0]):
        w = q[part, pl.ds(half_rows, 16), :].astype(f32)
        for pair in range(half_rows // queries // 2):
            s = dot(k, q[part, pl.ds(pair * 2 * queries, 2 * queries), :], NT)
            for u in range(2):
                row = pair * 2 + u
                total += jnp.maximum(s[:, u * queries : (u + 1) * queries], 0.0) * w[row : row + 1]
    acc[...] = total
    if first:
        return

    @pl.when(step == pl.num_programs(0) - 1)
    def _():
        vis = visible_mask(kp[...], qp[...])
        hidden = jnp.where(vis, acc[...] * scale, masked_floor)
        m = jnp.max(hidden, axis=0, keepdims=True)
        e = jnp.where(vis, jnp.exp(hidden - m), 0.0)
        e_out[...] = e
        z = jnp.sum(e, axis=0, keepdims=True)
        rows = lax.broadcasted_iota(jnp.int32, stats.shape, 0)
        stats[...] = jnp.where(rows == 0, m, z)


def logits_call(keys, q, before, kp, qp, scale, half_rows):
    n, width = keys.shape
    parts, rows, _ = q.shape
    queries = qp.shape[1]
    full = lambda a: pl.BlockSpec(a.shape, lambda d: (0, 0))
    first = before is None
    whole = pl.BlockSpec((n, queries), lambda d: (0, 0))
    args = [keys, q] + ([] if first else [before, kp, qp])
    specs = [full(keys), pl.BlockSpec((per_step, rows, width), lambda d: (d, 0, 0))]
    specs += [] if first else [full(before), full(kp), full(qp)]
    table = jax.ShapeDtypeStruct((n, queries), f32)
    return pl.pallas_call(
        functools.partial(logits_kernel, scale, half_rows, first),
        grid=(parts // per_step,),
        in_specs=specs,
        out_specs=whole if first else [whole, pl.BlockSpec((8, queries), lambda d: (0, 0))],
        out_shape=table if first else [table, jax.ShapeDtypeStruct((8, queries), f32)],
        scratch_shapes=[] if first else [pltpu.VMEM((n, queries), f32)],
        compiler_params=params(),
        cost_estimate=pl.CostEstimate(
            flops=2 * 2 * n * parts * half_rows * width,
            bytes_accessed=parts * rows * width * 2,
            transcendentals=0,
        ),
        name="logits",
    )(*args)


def lg_kernel(rec, e, own, stats, kp, qp, lg):
    n = e.shape[0]
    s = jnp.zeros(e.shape, f32)
    for i in range(rec.shape[0]):
        ex = from_code(rec[i, pl.ds(n, 16), :])
        rows, step = n // row_blocks, 16 // row_blocks
        parts = [
            root_decode(rec[i, pl.ds(b * rows, rows), :], ex[b * step : b * step + 1])
            for b in range(row_blocks)
        ]
        s += jnp.concatenate(parts, axis=0)
    every, queries = stats[:, 0, :], e.shape[1]
    m_all, z_all, t_all = (every[:, i * queries : (i + 1) * queries] for i in range(3))
    top = jnp.max(m_all, axis=0, keepdims=True)
    z = jnp.sum(z_all * jnp.exp(m_all - top), axis=0, keepdims=True)
    t = jnp.sum(t_all, axis=0, keepdims=True)
    p = e[...] * jnp.exp(own[0:1, :] - top) / z
    target = s / t
    lg[...] = loss_scale * jnp.where(visible_mask(kp[...], qp[...]), p - target, 0.0)


def lg_call(rec, e, own, stats, kp, qp):
    return pl.pallas_call(
        lg_kernel,
        out_shape=jax.ShapeDtypeStruct(e.shape, f32),
        compiler_params=params(),
        cost_estimate=pl.CostEstimate(flops=8 * rec.size, bytes_accessed=2 * rec.size, transcendentals=0),
        name="logit_grad",
    )(rec, e, own, stats, kp, qp)


def grads_kernel(scale, half_rows, sides, sums, more, gk_out, gk_more, which, keys, lg_ref, *refs):
    refs = list(refs)
    take = lambda count: [refs.pop(0) for _ in range(count)]
    qs = take(sides)
    befores = take(sides if more else 0)
    gk_in = take(1)[0] if gk_more else None
    outs = take(sides if sums else 0)
    gk = take(1)[0] if gk_out else None
    keys_t = take(1)[0]
    queries = lg_ref.shape[1]
    width = keys.shape[1]
    half = width // 2

    @pl.when(pl.program_id(0) == 0)
    def _():
        if gk_out:
            gk[...] = gk_in[...] if gk_more else jnp.zeros(gk.shape, f32)
        keys_t[...] = jnp.transpose(keys[...])

    k = keys[...]
    lg = lg_ref[...]
    heads = half_rows // queries
    for side in range(sides):
        q = qs[side]
        for part in range(q.shape[1]):
            w = q[0, part, pl.ds(half_rows, 16), :].astype(f32) * scale
            qp = q[0, part, pl.ds(0, half_rows), :]
            s = dot(k, qp, NT)
            cut = lambda x, u: x[:, u * queries : (u + 1) * queries]
            pres = [
                jnp.where(cut(s, u) > 0.0, w[u : u + 1] * lg, 0.0).astype(bf16) for u in range(heads)
            ]
            pre = jnp.concatenate(pres, axis=1)
            if gk_out:
                gk[...] += dot(pre, qp)
            if not sums:
                continue
            gq = dot(keys_t[...], pre)
            for u in range(heads):
                gw = scale * jnp.sum(jnp.maximum(cut(s, u), 0.0) * lg, axis=0, keepdims=True)
                for v in range(2):
                    at = (part * heads + u) * 2 + v
                    block = cut(gq, u)[v * half : (v + 1) * half]
                    row = jnp.broadcast_to(gw, (8, queries))
                    if more:
                        block += befores[side][at, pl.ds(0, half), :]
                        row += befores[side][at, pl.ds(half, 8), :]
                    outs[side][at, pl.ds(0, half), :] = block
                    outs[side][at, pl.ds(half, 8), :] = row


def grads_call(which, keys, lg, qs, befores, gk_out, gk_in, scale, half_rows, sums=True):
    n, width = keys.shape
    parts, rows, _ = qs[0].shape
    queries = lg.shape[1]
    blocks = 2 * half_rows // queries * grads_step
    steps = parts // 2 // grads_step
    full = lambda a: pl.BlockSpec(a.shape, lambda d, z: (0, 0))
    part = pl.BlockSpec((1, grads_step, rows, width), lambda d, z: (z[0], d, 0, 0))
    out = pl.BlockSpec((blocks, width // 2 + 8, queries), lambda d, z: (d, 0, 0))
    more, gk_more = befores is not None, gk_in is not None
    args = [keys, lg] + [q.reshape(2, parts // 2, rows, width) for q in qs]
    args += (befores if more else []) + ([gk_in] if gk_more else [])
    specs = [full(keys), full(lg)] + [part] * len(qs)
    specs += [out] * len(qs) if more else []
    specs += [full(gk_in)] if gk_more else []
    table = jax.ShapeDtypeStruct((steps * blocks, width // 2 + 8, queries), f32)
    given = len(qs) if sums else 0
    return pl.pallas_call(
        functools.partial(grads_kernel, scale, half_rows, len(qs), sums, more, gk_out, gk_more),
        grid_spec=pltpu.PrefetchScalarGridSpec(
            num_scalar_prefetch=1,
            grid=(steps,),
            in_specs=specs,
            out_specs=[out] * given + [pl.BlockSpec((n, width), lambda d, z: (0, 0))] * gk_out,
            scratch_shapes=[pltpu.VMEM((width, n), bf16)],
        ),
        out_shape=[table] * given + [jax.ShapeDtypeStruct((n, width), f32)] * gk_out,
        compiler_params=params(),
        cost_estimate=pl.CostEstimate(
            flops=3 * n * parts * len(qs) * half_rows * width,
            bytes_accessed=parts * len(qs) * rows * width * 3,
            transcendentals=0,
        ),
        name="grads",
    )(which, *args)


def code_kernel(a, b, out):
    x = a[...] + b[...]
    half = x.shape[1] - 8
    queries = x.shape[2]
    for i in range(x.shape[0]):
        g = x[i, 0:half]
        e = exponent(jnp.max(jnp.abs(g), axis=0, keepdims=True))
        out[i, pl.ds(0, half), :] = to_code(shrink(g, e) * 32767.0)
        w = x[i, half : half + 8]
        ew = exponent(jnp.abs(w))
        fine = shrink(w, ew) * 32767.0
        hi = jnp.floor(fine + 0.5)
        lo = (fine - hi) * 65534.0
        e16 = jnp.broadcast_to(e, (16, queries))
        spare = jnp.concatenate([ew, ew], axis=0)
        row = lax.broadcasted_iota(jnp.int32, (16, queries), 0)
        spare = jnp.where(row == 0, e16, spare)
        spare = jnp.where(row == 2, jnp.concatenate([hi, hi], axis=0), spare)
        spare = jnp.where(row == 3, jnp.concatenate([lo, lo], axis=0), spare)
        out[i, pl.ds(half, 16), :] = to_code(spare)


def code_call(a, b, parts):
    n, rows, queries = a.shape
    per = n // parts
    spec = pl.BlockSpec((per, rows, queries), lambda d: (d, 0, 0))
    return pl.pallas_call(
        code_kernel,
        grid=(parts,),
        in_specs=[spec, spec],
        out_specs=pl.BlockSpec((per, rows + 8, queries), lambda d: (d, 0, 0)),
        out_shape=jax.ShapeDtypeStruct((n, rows + 8, queries), jnp.int16),
        compiler_params=params(),
        name="code_parts",
    )(a, b)


def sum_kernel(rec, out):
    half = rec.shape[1] - 16
    queries = rec.shape[2]
    g = jnp.zeros((half, queries), f32)
    w = jnp.zeros((1, queries), f32)
    for i in range(rec.shape[0]):
        spare = from_code(rec[i, pl.ds(half, 16), :])
        g += grow(from_code(rec[i, pl.ds(0, half), :]) * (1.0 / 32767.0), spare[0:1])
        w += grow((spare[2:3] + spare[3:4] * (1.0 / 65534.0)) * (1.0 / 32767.0), spare[1:2])
    for i in range(out.shape[0]):
        out[i, pl.ds(0, half), :] = g
        out[i, pl.ds(half, 8), :] = jnp.broadcast_to(w, (8, queries))


def sum_call(rec, copies):
    n, rows, queries = rec.shape
    return pl.pallas_call(
        sum_kernel,
        out_shape=jax.ShapeDtypeStruct((copies, rows - 8, queries), f32),
        compiler_params=params(),
        name="sum_parts",
    )(rec)


def place_kernel(core, mine, other, gq, gw):
    heads, _, width = gq.shape
    half = width // 2
    for j in range(heads):
        side, jj = j // (heads // 2), j % (heads // 2)
        own = core[0] == side
        pick = lambda i: jnp.where(own, mine[i], other[i])
        lo, hi = pick(2 * jj), pick(2 * jj + 1)
        gq[j] = jnp.transpose(jnp.concatenate([lo[0:half], hi[0:half]], axis=0))
        gw[pl.ds(j, 1), :] = lo[half : half + 1]


def place_call(core, mine, other, heads, width):
    queries = mine.shape[2]
    vmem = pl.BlockSpec(memory_space=pltpu.VMEM)
    return pl.pallas_call(
        place_kernel,
        in_specs=[pl.BlockSpec(memory_space=pltpu.SMEM), vmem, vmem],
        out_specs=[vmem, vmem],
        out_shape=[
            jax.ShapeDtypeStruct((heads, queries, width), f32),
            jax.ShapeDtypeStruct((heads, queries), f32),
        ],
        compiler_params=params(),
        name="place",
    )(core.reshape(1), mine, other)


def spread(x, axes, count):
    return lax.all_to_all(jnp.broadcast_to(x[None], (count,) + x.shape), axes, 0, 0, tiled=True)


HEAD = ("zh", "x")
ZY = ("zl", "y")
CORE = ("core",)


def per_device(
    mla_queries,
    latent_cache,
    normalizers,
    query_positions,
    key_positions,
    index_queries,
    index_keys,
    index_weights,
):
    query_count = mla_queries.shape[1]
    sub_keys, index_width = index_keys.shape
    parts = lax.axis_size(HEAD)
    zy = lax.axis_size(ZY)
    local_heads = index_queries.shape[0]
    half_heads = local_heads // 2
    half_rows = half_heads * query_count
    index_scale = (local_heads * parts * index_width) ** (-0.5)
    core = lax.axis_index("core")
    swap = [(0, 1), (1, 0)]
    qp = query_positions.reshape(1, query_count)

    own_q = lax.dynamic_slice_in_dim(index_queries, core * half_heads, half_heads, 0)
    own_w = lax.dynamic_slice_in_dim(index_weights, core * half_heads, half_heads, 0)
    own = jnp.concatenate(
        [
            own_q.reshape(half_rows, index_width),
            jnp.pad(own_w, ((0, 16 - half_heads), (0, 0))),
        ],
        axis=0,
    )
    q_mine = spread(own, HEAD, parts)
    coded, total = probs_call(
        latent_cache.T, mla_queries.transpose(0, 2, 1), normalizers, key_positions, qp, parts
    )
    pair_keys = lax.ppermute(index_keys, "zh", swap)
    q_mine, coded, pair_keys = lax.optimization_barrier((q_mine, coded, pair_keys))
    q_other = lax.ppermute(q_mine, "core", swap)
    rec = lax.all_to_all(coded, HEAD, 0, 0, tiled=True)

    offset = lax.axis_index(HEAD) * sub_keys
    own_kp = lax.dynamic_slice_in_dim(key_positions, offset, sub_keys, 0).reshape(1, sub_keys)
    acc = logits_call(index_keys, q_mine, None, own_kp, qp, index_scale, half_rows)
    e, local = logits_call(index_keys, q_other, acc, own_kp, qp, index_scale, half_rows)
    stats = jnp.concatenate([local[0:1], local[1:2], total[0:1]], axis=1)
    side = lax.axis_index("zh").reshape(1)
    stats, rec, side, far = lax.optimization_barrier((stats, rec, side, 1 - side))
    stats = spread(stats, HEAD + ZY + CORE, parts * zy * 2)
    lg = lg_call(rec, e, local, stats, own_kp, qp)

    pair_lg = lax.ppermute(lg, "zh", swap)
    grads = functools.partial(grads_call, scale=index_scale, half_rows=half_rows)
    own_other, own_mine, gk = grads(side, index_keys, lg, [q_other, q_mine], None, True, None)
    (gk,) = grads(far, index_keys, lg, [q_other, q_mine], None, True, gk, sums=False)
    (own_other, own_mine, gk, pair_lg) = lax.optimization_barrier((own_other, own_mine, gk, pair_lg))
    (out_other,) = grads(side, pair_keys, pair_lg, [q_other], [own_other], False, None)
    got = lax.ppermute(out_other, "core", swap)
    (out_mine,) = grads(side, pair_keys, pair_lg, [q_mine], [own_mine], False, None)
    block = lax.all_to_all(code_call(out_mine, got, parts // 2), ("x",) + ZY, 0, 0, tiled=True)
    mine = lax.all_to_all(sum_call(block, zy), ZY, 0, 0, tiled=True)
    other = lax.ppermute(mine, "core", swap)
    gq, gw = place_call(core, mine, other, local_heads, index_width)
    return gq, gw, gk


def solution(mesh):
    fine = Mesh(mesh.devices.reshape(2, 4, 2, 4, 2), HEAD + ZY + ("core",))
    ctx = ZY + ("core",)
    placed = (
        P(HEAD, None, None),
        P(ctx, None),
        P(HEAD, None),
        P(),
        P(ctx),
        P(HEAD, None, None),
        P(ctx + HEAD, None),
        P(HEAD, None),
    )
    return jax.shard_map(
        per_device,
        mesh=fine,
        in_specs=placed,
        out_specs=(P(HEAD, None, None), P(HEAD, None), P(ctx + HEAD, None)),
        check_vma=False,
    )
```

```python
import functools
import math

import jax
import jax.numpy as jnp
from jax import lax
from jax.experimental import pallas as pl
from jax.experimental.pallas import tpu as pltpu
from jax.sharding import Mesh
from jax.sharding import PartitionSpec as P

att_scale = 192.0 ** (-0.5)
loss_scale = 1024.0
masked_floor = -1e30
log2e = math.log2(math.e)
per_step = 4
grads_step = 4
row_blocks = 4

NT = (((1,), (1,)), ((), ()))
NN = (((1,), (0,)), ((), ()))
f32 = jnp.float32
bf16 = jnp.bfloat16


def dot(a, b, dims=NN):
    return lax.dot_general(a, b, dims, preferred_element_type=f32)


def visible_mask(kp_row, qp_row):
    n = kp_row.shape[1]
    q = qp_row.shape[1]
    kp = jnp.transpose(jnp.broadcast_to(kp_row, (q, n)))
    return kp <= jnp.broadcast_to(qp_row, (n, q))


def params(mb=20):
    return pltpu.CompilerParams(vmem_limit_bytes=mb * 1024 * 1024)


def exponent(top):
    return jnp.clip(jnp.ceil(jnp.log2(jnp.maximum(top, 1e-37))), -122.0, 128.0)


def shrink(x, e):
    r = jnp.exp2(e * -0.5)
    return (x * r) * r


def grow(x, e):
    r = jnp.exp2(e * 0.5)
    return (x * r) * r


def to_code(x):
    return jnp.clip(jnp.floor(x + 0.5), -32768.0, 32767.0).astype(jnp.int32).astype(jnp.int16)


def from_code(c):
    return c.astype(jnp.int32).astype(f32)


def root_code(x, e):
    root = jnp.where(x > 0.0, lax.rsqrt(lax.rsqrt(x)), 0.0)
    return ((root * (65535.0 * jnp.exp2(e * -0.25)) + 0.5).astype(jnp.int32) - 32768).astype(jnp.int16)


def root_decode(c, e):
    r = (from_code(c) + 32768.0) * (1.0 / 65535.0) * jnp.exp2(e * 0.25)
    r = r * r
    return r * r


def probs_kernel(cache, q, nrm, kp, qp, out, tot):
    keys = cache.shape[1]
    heads, queries = nrm.shape

    @pl.when(pl.program_id(0) == 0)
    def _():
        tot[...] = jnp.zeros(tot.shape, f32)

    rows = keys // row_blocks
    e_rows = []
    total = jnp.zeros((1, queries), f32)
    for block in range(row_blocks):
        x = jnp.transpose(cache[:, pl.ds(block * rows, rows)])
        acc = jnp.zeros((rows, queries), f32)
        for pair in range(heads // 2):
            s = dot(x, jnp.concatenate([q[pair * 2], q[pair * 2 + 1]], axis=1))
            for u in range(2):
                n = nrm[pl.ds(pair * 2 + u, 1), :] * log2e
                acc += jnp.exp2(s[:, u * queries : (u + 1) * queries] * (att_scale * log2e) - n)
        acc = jnp.where(visible_mask(kp[0, :, pl.ds(block * rows, rows)], qp[...]), acc, 0.0)
        e = exponent(jnp.max(acc, axis=0, keepdims=True))
        out[0, pl.ds(block * rows, rows), :] = root_code(acc, e)
        e_rows.append(jnp.broadcast_to(e, (16 // row_blocks, queries)))
        total += jnp.sum(acc, axis=0, keepdims=True)
    out[0, pl.ds(keys, 16), :] = to_code(jnp.concatenate(e_rows, axis=0))
    tot[...] += jnp.broadcast_to(total, tot.shape)


def probs_call(cache_t, q_t, nrm, kp, qp, parts):
    width, keys = cache_t.shape
    rows = keys // parts
    heads, queries = nrm.shape
    return pl.pallas_call(
        probs_kernel,
        grid=(parts,),
        in_specs=[
            pl.BlockSpec((width, rows), lambda d: (0, d)),
            pl.BlockSpec(q_t.shape, lambda d: (0, 0, 0)),
            pl.BlockSpec(nrm.shape, lambda d: (0, 0)),
            pl.BlockSpec((1, 1, rows), lambda d: (d, 0, 0)),
            pl.BlockSpec(qp.shape, lambda d: (0, 0)),
        ],
        out_specs=[
            pl.BlockSpec((1, rows + 16, queries), lambda d: (d, 0, 0)),
            pl.BlockSpec((8, queries), lambda d: (0, 0)),
        ],
        out_shape=[
            jax.ShapeDtypeStruct((parts, rows + 16, queries), jnp.int16),
            jax.ShapeDtypeStruct((8, queries), f32),
        ],
        compiler_params=params(56),
        cost_estimate=pl.CostEstimate(
            flops=2 * keys * q_t.size,
            bytes_accessed=cache_t.size * 2 + q_t.size * 2,
            transcendentals=keys * heads * queries,
        ),
        name="probs",
    )(cache_t, q_t, nrm, kp.reshape(parts, 1, rows), qp)


def logits_kernel(scale, half_rows, first, *refs):
    if first:
        keys, q, acc = refs
    else:
        keys, q, before, kp, qp, e_out, stats, acc = refs
    queries = acc.shape[1]
    step = pl.program_id(0)

    @pl.when(step == 0)
    def _():
        acc[...] = jnp.zeros(acc.shape, f32) if first else before[...]

    k = keys[...]
    total = acc[...]
    for part in range(q.shape[0]):
        w = q[part, pl.ds(half_rows, 16), :].astype(f32)
        for pair in range(half_rows // queries // 2):
            s = dot(k, q[part, pl.ds(pair * 2 * queries, 2 * queries), :], NT)
            for u in range(2):
                row = pair * 2 + u
                total += jnp.maximum(s[:, u * queries : (u + 1) * queries], 0.0) * w[row : row + 1]
    acc[...] = total
    if first:
        return

    @pl.when(step == pl.num_programs(0) - 1)
    def _():
        vis = visible_mask(kp[...], qp[...])
        hidden = jnp.where(vis, acc[...] * scale, masked_floor)
        m = jnp.max(hidden, axis=0, keepdims=True)
        e = jnp.where(vis, jnp.exp(hidden - m), 0.0)
        e_out[...] = e
        z = jnp.sum(e, axis=0, keepdims=True)
        rows = lax.broadcasted_iota(jnp.int32, stats.shape, 0)
        stats[...] = jnp.where(rows == 0, m, z)


def logits_call(keys, q, before, kp, qp, scale, half_rows):
    n, width = keys.shape
    parts, rows, _ = q.shape
    queries = qp.shape[1]
    full = lambda a: pl.BlockSpec(a.shape, lambda d: (0, 0))
    first = before is None
    whole = pl.BlockSpec((n, queries), lambda d: (0, 0))
    args = [keys, q] + ([] if first else [before, kp, qp])
    specs = [full(keys), pl.BlockSpec((per_step, rows, width), lambda d: (d, 0, 0))]
    specs += [] if first else [full(before), full(kp), full(qp)]
    table = jax.ShapeDtypeStruct((n, queries), f32)
    return pl.pallas_call(
        functools.partial(logits_kernel, scale, half_rows, first),
        grid=(parts // per_step,),
        in_specs=specs,
        out_specs=whole if first else [whole, pl.BlockSpec((8, queries), lambda d: (0, 0))],
        out_shape=table if first else [table, jax.ShapeDtypeStruct((8, queries), f32)],
        scratch_shapes=[] if first else [pltpu.VMEM((n, queries), f32)],
        compiler_params=params(),
        cost_estimate=pl.CostEstimate(
            flops=2 * 2 * n * parts * half_rows * width,
            bytes_accessed=parts * rows * width * 2,
            transcendentals=0,
        ),
        name="logits",
    )(*args)


def lg_kernel(rec, e, own, stats, kp, qp, lg):
    n = e.shape[0]
    s = jnp.zeros(e.shape, f32)
    for i in range(rec.shape[0]):
        ex = from_code(rec[i, pl.ds(n, 16), :])
        rows, step = n // row_blocks, 16 // row_blocks
        parts = [
            root_decode(rec[i, pl.ds(b * rows, rows), :], ex[b * step : b * step + 1])
            for b in range(row_blocks)
        ]
        s += jnp.concatenate(parts, axis=0)
    every, queries = stats[:, 0, :], e.shape[1]
    m_all, z_all, t_all = (every[:, i * queries : (i + 1) * queries] for i in range(3))
    top = jnp.max(m_all, axis=0, keepdims=True)
    z = jnp.sum(z_all * jnp.exp(m_all - top), axis=0, keepdims=True)
    t = jnp.sum(t_all, axis=0, keepdims=True)
    p = e[...] * jnp.exp(own[0:1, :] - top) / z
    target = s / t
    lg[...] = loss_scale * jnp.where(visible_mask(kp[...], qp[...]), p - target, 0.0)


def lg_call(rec, e, own, stats, kp, qp):
    return pl.pallas_call(
        lg_kernel,
        out_shape=jax.ShapeDtypeStruct(e.shape, f32),
        compiler_params=params(),
        cost_estimate=pl.CostEstimate(flops=8 * rec.size, bytes_accessed=2 * rec.size, transcendentals=0),
        name="logit_grad",
    )(rec, e, own, stats, kp, qp)


def grads_kernel(scale, half_rows, sides, sums, more, gk_out, gk_more, which, keys, lg_ref, *refs):
    refs = list(refs)
    take = lambda count: [refs.pop(0) for _ in range(count)]
    qs = take(sides)
    befores = take(sides if more else 0)
    gk_in = take(1)[0] if gk_more else None
    outs = take(sides if sums else 0)
    gk = take(1)[0] if gk_out else None
    keys_t = take(1)[0]
    queries = lg_ref.shape[1]
    width = keys.shape[1]
    half = width // 2

    @pl.when(pl.program_id(0) == 0)
    def _():
        if gk_out:
            gk[...] = gk_in[...] if gk_more else jnp.zeros(gk.shape, f32)
        keys_t[...] = jnp.transpose(keys[...])

    k = keys[...]
    lg = lg_ref[...]
    heads = half_rows // queries
    for side in range(sides):
        q = qs[side]
        for part in range(q.shape[1]):
            w = q[0, part, pl.ds(half_rows, 16), :].astype(f32) * scale
            qp = q[0, part, pl.ds(0, half_rows), :]
            s = dot(k, qp, NT)
            cut = lambda x, u: x[:, u * queries : (u + 1) * queries]
            pres = [
                jnp.where(cut(s, u) > 0.0, w[u : u + 1] * lg, 0.0).astype(bf16) for u in range(heads)
            ]
            pre = jnp.concatenate(pres, axis=1)
            if gk_out:
                gk[...] += dot(pre, qp)
            if not sums:
                continue
            gq = dot(keys_t[...], pre)
            for u in range(heads):
                gw = scale * jnp.sum(jnp.maximum(cut(s, u), 0.0) * lg, axis=0, keepdims=True)
                for v in range(2):
                    at = (part * heads + u) * 2 + v
                    block = cut(gq, u)[v * half : (v + 1) * half]
                    row = jnp.broadcast_to(gw, (8, queries))
                    if more:
                        block += befores[side][at, pl.ds(0, half), :]
                        row += befores[side][at, pl.ds(half, 8), :]
                    outs[side][at, pl.ds(0, half), :] = block
                    outs[side][at, pl.ds(half, 8), :] = row


def grads_call(which, keys, lg, qs, befores, gk_out, gk_in, scale, half_rows, sums=True):
    n, width = keys.shape
    parts, rows, _ = qs[0].shape
    queries = lg.shape[1]
    blocks = 2 * half_rows // queries * grads_step
    steps = parts // 2 // grads_step
    full = lambda a: pl.BlockSpec(a.shape, lambda d, z: (0, 0))
    part = pl.BlockSpec((1, grads_step, rows, width), lambda d, z: (z[0], d, 0, 0))
    out = pl.BlockSpec((blocks, width // 2 + 8, queries), lambda d, z: (d, 0, 0))
    more, gk_more = befores is not None, gk_in is not None
    args = [keys, lg] + [q.reshape(2, parts // 2, rows, width) for q in qs]
    args += (befores if more else []) + ([gk_in] if gk_more else [])
    specs = [full(keys), full(lg)] + [part] * len(qs)
    specs += [out] * len(qs) if more else []
    specs += [full(gk_in)] if gk_more else []
    table = jax.ShapeDtypeStruct((steps * blocks, width // 2 + 8, queries), f32)
    given = len(qs) if sums else 0
    return pl.pallas_call(
        functools.partial(grads_kernel, scale, half_rows, len(qs), sums, more, gk_out, gk_more),
        grid_spec=pltpu.PrefetchScalarGridSpec(
            num_scalar_prefetch=1,
            grid=(steps,),
            in_specs=specs,
            out_specs=[out] * given + [pl.BlockSpec((n, width), lambda d, z: (0, 0))] * gk_out,
            scratch_shapes=[pltpu.VMEM((width, n), bf16)],
        ),
        out_shape=[table] * given + [jax.ShapeDtypeStruct((n, width), f32)] * gk_out,
        compiler_params=params(),
        cost_estimate=pl.CostEstimate(
            flops=3 * n * parts * len(qs) * half_rows * width,
            bytes_accessed=parts * len(qs) * rows * width * 3,
            transcendentals=0,
        ),
        name="grads",
    )(which, *args)


def code_kernel(a, b, out):
    x = a[...] + b[...]
    half = x.shape[1] - 8
    queries = x.shape[2]
    for i in range(x.shape[0]):
        g = x[i, 0:half]
        e = exponent(jnp.max(jnp.abs(g), axis=0, keepdims=True))
        out[i, pl.ds(0, half), :] = to_code(shrink(g, e) * 32767.0)
        w = x[i, half : half + 8]
        ew = exponent(jnp.abs(w))
        fine = shrink(w, ew) * 32767.0
        hi = jnp.floor(fine + 0.5)
        lo = (fine - hi) * 65534.0
        e16 = jnp.broadcast_to(e, (16, queries))
        spare = jnp.concatenate([ew, ew], axis=0)
        row = lax.broadcasted_iota(jnp.int32, (16, queries), 0)
        spare = jnp.where(row == 0, e16, spare)
        spare = jnp.where(row == 2, jnp.concatenate([hi, hi], axis=0), spare)
        spare = jnp.where(row == 3, jnp.concatenate([lo, lo], axis=0), spare)
        out[i, pl.ds(half, 16), :] = to_code(spare)


def code_call(a, b, parts):
    n, rows, queries = a.shape
    per = n // parts
    spec = pl.BlockSpec((per, rows, queries), lambda d: (d, 0, 0))
    return pl.pallas_call(
        code_kernel,
        grid=(parts,),
        in_specs=[spec, spec],
        out_specs=pl.BlockSpec((per, rows + 8, queries), lambda d: (d, 0, 0)),
        out_shape=jax.ShapeDtypeStruct((n, rows + 8, queries), jnp.int16),
        compiler_params=params(),
        name="code_parts",
    )(a, b)


def sum_kernel(rec, out):
    half = rec.shape[1] - 16
    queries = rec.shape[2]
    g = jnp.zeros((half, queries), f32)
    w = jnp.zeros((1, queries), f32)
    for i in range(rec.shape[0]):
        spare = from_code(rec[i, pl.ds(half, 16), :])
        g += grow(from_code(rec[i, pl.ds(0, half), :]) * (1.0 / 32767.0), spare[0:1])
        w += grow((spare[2:3] + spare[3:4] * (1.0 / 65534.0)) * (1.0 / 32767.0), spare[1:2])
    for i in range(out.shape[0]):
        out[i, pl.ds(0, half), :] = g
        out[i, pl.ds(half, 8), :] = jnp.broadcast_to(w, (8, queries))


def sum_call(rec, copies):
    n, rows, queries = rec.shape
    return pl.pallas_call(
        sum_kernel,
        out_shape=jax.ShapeDtypeStruct((copies, rows - 8, queries), f32),
        compiler_params=params(),
        name="sum_parts",
    )(rec)


def place_kernel(core, mine, other, gq, gw):
    heads, _, width = gq.shape
    half = width // 2
    for j in range(heads):
        side, jj = j // (heads // 2), j % (heads // 2)
        own = core[0] == side
        pick = lambda i: jnp.where(own, mine[i], other[i])
        lo, hi = pick(2 * jj), pick(2 * jj + 1)
        gq[j] = jnp.transpose(jnp.concatenate([lo[0:half], hi[0:half]], axis=0))
        gw[pl.ds(j, 1), :] = lo[half : half + 1]


def place_call(core, mine, other, heads, width):
    queries = mine.shape[2]
    vmem = pl.BlockSpec(memory_space=pltpu.VMEM)
    return pl.pallas_call(
        place_kernel,
        in_specs=[pl.BlockSpec(memory_space=pltpu.SMEM), vmem, vmem],
        out_specs=[vmem, vmem],
        out_shape=[
            jax.ShapeDtypeStruct((heads, queries, width), f32),
            jax.ShapeDtypeStruct((heads, queries), f32),
        ],
        compiler_params=params(),
        name="place",
    )(core.reshape(1), mine, other)


def spread(x, axes, count):
    return lax.all_to_all(jnp.broadcast_to(x[None], (count,) + x.shape), axes, 0, 0, tiled=True)


HEAD = ("zh", "x")
ZY = ("zl", "y")
CORE = ("core",)


def per_device(
    mla_queries,
    latent_cache,
    normalizers,
    query_positions,
    key_positions,
    index_queries,
    index_keys,
    index_weights,
):
    query_count = mla_queries.shape[1]
    sub_keys, index_width = index_keys.shape
    parts = lax.axis_size(HEAD)
    zy = lax.axis_size(ZY)
    local_heads = index_queries.shape[0]
    half_heads = local_heads // 2
    half_rows = half_heads * query_count
    index_scale = (local_heads * parts * index_width) ** (-0.5)
    core = lax.axis_index("core")
    swap = [(0, 1), (1, 0)]
    qp = query_positions.reshape(1, query_count)

    own_q = lax.dynamic_slice_in_dim(index_queries, core * half_heads, half_heads, 0)
    own_w = lax.dynamic_slice_in_dim(index_weights, core * half_heads, half_heads, 0)
    own = jnp.concatenate(
        [
            own_q.reshape(half_rows, index_width),
            jnp.pad(own_w, ((0, 16 - half_heads), (0, 0))),
        ],
        axis=0,
    )
    q_mine = spread(own, HEAD, parts)
    coded, total = probs_call(
        latent_cache.T, mla_queries.transpose(0, 2, 1), normalizers, key_positions, qp, parts
    )
    pair_keys = lax.ppermute(index_keys, "zh", swap)
    q_mine, coded, pair_keys = lax.optimization_barrier((q_mine, coded, pair_keys))
    q_other = lax.ppermute(q_mine, "core", swap)
    rec = lax.all_to_all(coded, HEAD, 0, 0, tiled=True)

    offset = lax.axis_index(HEAD) * sub_keys
    own_kp = lax.dynamic_slice_in_dim(key_positions, offset, sub_keys, 0).reshape(1, sub_keys)
    acc = logits_call(index_keys, q_mine, None, own_kp, qp, index_scale, half_rows)
    e, local = logits_call(index_keys, q_other, acc, own_kp, qp, index_scale, half_rows)
    stats = jnp.concatenate([local[0:1], local[1:2], total[0:1]], axis=1)
    side = lax.axis_index("zh").reshape(1)
    stats, rec, side, far = lax.optimization_barrier((stats, rec, side, 1 - side))
    stats = spread(stats, HEAD + ZY + CORE, parts * zy * 2)
    lg = lg_call(rec, e, local, stats, own_kp, qp)

    pair_lg = lax.ppermute(lg, "zh", swap)
    grads = functools.partial(grads_call, scale=index_scale, half_rows=half_rows)
    own_other, own_mine, gk = grads(side, index_keys, lg, [q_other, q_mine], None, True, None)
    (gk,) = grads(far, index_keys, lg, [q_other, q_mine], None, True, gk, sums=False)
    (own_other, own_mine, gk, pair_lg) = lax.optimization_barrier((own_other, own_mine, gk, pair_lg))
    (out_other,) = grads(side, pair_keys, pair_lg, [q_other], [own_other], False, None)
    got = lax.ppermute(out_other, "core", swap)
    (out_mine,) = grads(side, pair_keys, pair_lg, [q_mine], [own_mine], False, None)
    block = lax.all_to_all(code_call(out_mine, got, parts // 2), ("x",) + ZY, 0, 0, tiled=True)
    mine = lax.all_to_all(sum_call(block, zy), ZY, 0, 0, tiled=True)
    other = lax.ppermute(mine, "core", swap)
    gq, gw = place_call(core, mine, other, local_heads, index_width)
    return gq, gw, gk


def solution(mesh):
    fine = Mesh(mesh.devices.reshape(2, 4, 2, 4, 2), HEAD + ZY + ("core",))
    ctx = ZY + ("core",)
    placed = (
        P(HEAD, None, None),
        P(ctx, None),
        P(HEAD, None),
        P(),
        P(ctx),
        P(HEAD, None, None),
        P(ctx + HEAD, None),
        P(HEAD, None),
    )
    return jax.shard_map(
        per_device,
        mesh=fine,
        in_specs=placed,
        out_specs=(P(HEAD, None, None), P(HEAD, None), P(ctx + HEAD, None)),
        check_vma=False,
    )
```
